32 devices in a mesh: groups: 2 (over y), ta: 4 (over z), gz: 2 (over x), gy: 2 (over core).
Axes of the slice: x: 2, y: 2, z: 4, core: 2. Of those that a mesh axis runs over, the one named last changes fastest.
Arguments:
- pseudo: float32 [64, 8, 8, 512], P('groups', 'ta', 'gz', 'gy'), parts along dimension 0, may hold values from -12 to 12
- frame_quat: float32 [32, 8, 8, 512], P('groups', 'ta', 'gz', 'gy'), parts along dimension 0, may hold values from -1 to 1, as said below
- link_phase: float32 [8, 8, 8, 512], P('groups', 'ta', 'gz', 'gy'), parts along dimension 0, may hold values from -3.140625 to 3.140625
- active: int32 [16, 8, 512], P(('groups', 'ta'), 'gz', 'gy'), parts along dimension 0, may hold values 0 or 1
- kernel: float32 [648, 16], replicated, may hold values from -0.25 to 0.25
- bias_hidden: float32 [16], replicated, may hold values from -3 to 3
- readout: float32 [16, 8], replicated, may hold values from -1.5 to 1.5
- bias_out: float32 [8], replicated, may hold values from -3 to 3
Outputs:
- solution: float32 [64, 8, 8, 512], P('groups', 'ta', 'gz', 'gy'), parts along dimension 0
- force_field: float32 [16, 8, 512], P(('groups', 'ta'), 'gz', 'gy'), parts along dimension 0
- grad_kernel: float32 [1296, 16], P('groups'), parts along dimension 0
- grad_hidden: float32 [32], P('groups'), parts along dimension 0
- grad_readout: float32 [32, 8], P('groups'), parts along dimension 0
- grad_out: float32 [16], P('groups'), parts along dimension 0
The draws below stay inside these ranges and needn't reach their ends.
There are 2 independent parts, one for each index of `groups`. The reference program is written for one: setup_inputs(seed, part) draws one part's arguments, and reference() takes and returns one part's arrays. A program takes and returns all parts, laid end to end along the dimension named above; an argument that names none is the same for every part. Nothing has to cross between parts.
Inputs may be any that keep to these rules, and one draw needn't show every extreme that they name: For every site and direction mu the four entries frame_quat[4 mu + j], j = 0..3, have a unit sum of squares.
All inputs are finite; a program needn't handle non-finite values. No bound on the sum of `active` on one device may be relied on, other than what follows from the above.
Results may differ from the reference program's by a relative error of at most 0.0003.
Values sent between devices are 32-bit elements; how exact they have to be, the bound alone decides.
A program may use at most 128 MiB of HBM per device.

```python
import math
import jax
import jax.numpy as jnp
import numpy as np
from jax import lax

X_LEN = 32
ITERS = 3
KNOTS = 8
CHANNELS = 16
NT = 8
NZ = 8
NY = 16


def draw_pseudo(key, part):
    extent = (32, NT, NZ, NY * X_LEN)
    first_key, second_key = jax.random.split(key)
    time_level = (jnp.arange(NT, dtype=jnp.float32) / max(NT - 1, 1)).reshape((1, NT, 1, 1))
    roughness = jax.random.uniform(second_key, (1, NT, NZ, NY * X_LEN), jnp.float32)
    base_draw = jnp.clip(jax.random.normal(first_key, extent, jnp.float32), -6.0, 6.0)
    log_level = 0.5 * (time_level + roughness)
    return 0.2 * jnp.power(10.0, log_level) * base_draw


def draw_frame_quat(key, part):
    extent = (4, 4, NT, NZ, NY * X_LEN)
    raw_draw = jax.random.normal(key, extent, jnp.float32)
    length_sq = raw_draw[:, 0] ** 2 + raw_draw[:, 1] ** 2 + raw_draw[:, 2] ** 2 + raw_draw[:, 3] ** 2
    unit_draw = raw_draw / jnp.sqrt(length_sq + 1e-12)[:, None]
    return unit_draw.reshape((16, NT, NZ, NY * X_LEN))


def plant(values, stream_key, low, top_value):
    longest = values.shape.index(max(values.shape))
    spots = []
    for shift in (0, 1):
        where = [jax.random.randint(jax.random.fold_in(stream_key, axis), (), 0, length) for axis, length in enumerate(values.shape)]
        where[longest] = (where[longest] + shift) % values.shape[longest]
        spots.append(tuple(where))
    return values.at[spots[0]].set(low).at[spots[1]].set(top_value)


def centred(key, shape, deviation, limit, kind=jnp.bfloat16):
    entries = jax.random.normal(key, shape, jnp.float32) * deviation
    return jnp.minimum(jnp.maximum(entries, -limit), limit).astype(kind)


def setup_inputs(seed: int = 0, part: int = 0) -> dict:
    key_list = jax.random.split(jax.random.key(seed), 9)
    part_keys = jax.random.split(jax.random.fold_in(key_list[8], part), 9)
    pseudo = draw_pseudo(jax.random.fold_in(jax.random.fold_in(key_list[8], part), 71), part)
    frame_quat = draw_frame_quat(jax.random.fold_in(jax.random.fold_in(key_list[8], part), 71), part)
    link_phase = jnp.clip(jax.random.uniform(part_keys[2], (4, NT, NZ, NY * X_LEN), jnp.float32, -3.140625, 3.140625), -3.140625, 3.140625)
    active = plant((jax.random.randint(part_keys[3], (NT, NZ, NY * X_LEN), 0, 2) < 1).astype(jnp.int32), jax.random.fold_in(part_keys[3], 1), 0, 1)
    kernel = centred(key_list[4], (648, CHANNELS), 648 ** -0.5, 0.25, jnp.float32)
    bias_hidden = centred(key_list[5], (CHANNELS,), 1.0, 3.0, jnp.float32)
    readout = centred(key_list[6], (CHANNELS, KNOTS), CHANNELS ** -0.5, 1.5, jnp.float32)
    bias_out = centred(key_list[7], (KNOTS,), 1.0, 3.0, jnp.float32)
    return dict(pseudo=pseudo, frame_quat=frame_quat, link_phase=link_phase, active=active, kernel=kernel, bias_hidden=bias_hidden, readout=readout, bias_out=bias_out)


PRECISE = lax.Precision.HIGHEST
KAPPAS = (0.12, 0.1)
SLOPE_SHARE = 0.5

def corner_blocks(upper_right, lower_left):
    matrix = np.zeros((4, 4), dtype=complex)
    matrix[0:2, 2:4] = upper_right
    matrix[2:4, 0:2] = lower_left
    return matrix

def spin_tables():
    identity = np.eye(2, dtype=complex)
    paulis = [np.array([[0, 1], [1, 0]], dtype=complex), np.array([[0, -1j], [1j, 0]], dtype=complex), np.array([[1, 0], [0, -1]], dtype=complex)]
    gammas = [corner_blocks(identity, identity)]
    for pauli_index in (2, 1, 0):
        gammas.append(corner_blocks(-1j * paulis[pauli_index], 1j * paulis[pauli_index]))
    lookup = np.zeros((2, 4, 2, 4, 4))
    for direction in range(4):
        for side_index in range(2):
            projector = np.eye(4) + (2 * side_index - 1) * gammas[direction]
            lookup[side_index, direction, 0] = projector.real
            lookup[side_index, direction, 1] = projector.imag
    return lookup

def spin_apply(side_index, direction, vector):
    table = spin_tables()
    real_part = jnp.asarray(table[side_index, direction, 0], jnp.float32)
    imag_part = jnp.asarray(table[side_index, direction, 1], jnp.float32)
    vec_re = vector[:, :, :, 0]
    vec_im = vector[:, :, :, 1]
    out_re = jnp.einsum('ab,fb...->fa...', real_part, vec_re, precision=PRECISE) - jnp.einsum('ab,fb...->fa...', imag_part, vec_im, precision=PRECISE)
    out_im = jnp.einsum('ab,fb...->fa...', real_part, vec_im, precision=PRECISE) + jnp.einsum('ab,fb...->fa...', imag_part, vec_re, precision=PRECISE)
    return jnp.stack([out_re, out_im], axis=3)

def colour_apply(quadruple, vector, adjoint):
    alpha_re, alpha_im, beta_re, beta_im = (quadruple[0], quadruple[1], quadruple[2], quadruple[3])
    up_re, up_im = (vector[:, :, 0, 0], vector[:, :, 0, 1])
    low_re, low_im = (vector[:, :, 1, 0], vector[:, :, 1, 1])
    if adjoint:
        top_re = alpha_re * up_re + alpha_im * up_im - beta_re * low_re + beta_im * low_im
        top_im = alpha_re * up_im - alpha_im * up_re - beta_re * low_im - beta_im * low_re
        bottom_re = beta_re * up_re + beta_im * up_im + alpha_re * low_re - alpha_im * low_im
        bottom_im = beta_re * up_im - beta_im * up_re + alpha_re * low_im + alpha_im * low_re
    else:
        top_re = alpha_re * up_re - alpha_im * up_im + beta_re * low_re - beta_im * low_im
        top_im = alpha_re * up_im + alpha_im * up_re + beta_re * low_im + beta_im * low_re
        bottom_re = -(beta_re * up_re + beta_im * up_im) + alpha_re * low_re + alpha_im * low_im
        bottom_im = -(beta_re * up_im - beta_im * up_re) + alpha_re * low_im - alpha_im * low_re
    upper_row = jnp.stack([top_re, top_im], axis=2)
    lower_row = jnp.stack([bottom_re, bottom_im], axis=2)
    return jnp.stack([upper_row, lower_row], axis=2)

def along_rows(tensor, stride):
    positions = jnp.arange(tensor.shape[-1]) % X_LEN
    if stride > 0:
        return jnp.where(positions == X_LEN - 1, jnp.roll(tensor, X_LEN - 1, axis=-1), jnp.roll(tensor, -1, axis=-1))
    return jnp.where(positions == 0, jnp.roll(tensor, 1 - X_LEN, axis=-1), jnp.roll(tensor, 1, axis=-1))

def region_view(tensor, shift_t, shift_z, shift_y):
    span_t = tensor.shape[-3] - 2
    span_z = tensor.shape[-2] - 2
    span_yx = tensor.shape[-1] - 2 * X_LEN
    start_y = (1 + shift_y) * X_LEN
    return tensor[..., 1 + shift_t:1 + shift_t + span_t, 1 + shift_z:1 + shift_z + span_z, start_y:start_y + span_yx]

def wilson(spinor, gauge_ext, adjoint):
    vector = spinor.reshape((2, 4, 2, 2) + spinor.shape[1:])
    quaternions = gauge_ext.reshape((4, 4) + gauge_ext.shape[1:])
    centre = region_view(vector, 0, 0, 0)
    gauge_here = region_view(quaternions, 0, 0, 0)
    forward_side = 1 if adjoint else 0
    hopping = jnp.zeros_like(centre)
    for direction in range(4):
        if direction < 3:
            unit_step = [0, 0, 0]
            unit_step[direction] = 1
            ahead_vec = region_view(vector, unit_step[0], unit_step[1], unit_step[2])
            behind = region_view(vector, -unit_step[0], -unit_step[1], -unit_step[2])
            gauge_behind = region_view(quaternions[direction], -unit_step[0], -unit_step[1], -unit_step[2])
        else:
            ahead_vec = along_rows(centre, 1)
            behind = along_rows(centre, -1)
            gauge_behind = along_rows(gauge_here[direction], -1)
        forward = colour_apply(gauge_here[direction], ahead_vec, False)
        backward = colour_apply(gauge_behind, behind, True)
        hopping = hopping + spin_apply(forward_side, direction, forward) + spin_apply(1 - forward_side, direction, backward)
    kappas = jnp.asarray(KAPPAS, jnp.float32).reshape((2, 1, 1, 1, 1, 1, 1))
    result = centre - kappas * hopping
    return result.reshape((32,) + result.shape[4:])

def rotate_one(quadruple, theta_field):
    cosine = jnp.cos(theta_field)
    sine_part = jnp.sin(theta_field)
    return jnp.stack([cosine * quadruple[0] - sine_part * quadruple[1], cosine * quadruple[1] + sine_part * quadruple[0], cosine * quadruple[2] - sine_part * quadruple[3], cosine * quadruple[3] + sine_part * quadruple[2]], axis=0)

def rotate_links(frame_quat, angles):
    return jnp.concatenate([rotate_one(frame_quat[4 * direction:4 * direction + 4], angles[direction]) for direction in range(4)], axis=0)

def bspline(offsets):
    distance = jnp.abs(offsets)
    outer_part = jnp.maximum(2.0 - distance, 0.0)
    inner_part = jnp.maximum(1.0 - distance, 0.0)
    return (outer_part ** 3 - 4.0 * inner_part ** 3) / 6.0

def bspline_slope(offsets):
    distance = jnp.abs(offsets)
    outer_part = jnp.maximum(2.0 - distance, 0.0)
    inner_part = jnp.maximum(1.0 - distance, 0.0)
    return jnp.sign(offsets) * (4.0 * inner_part ** 2 - outer_part ** 2) / 2.0

def spline_basis(time_angle):
    position = KNOTS * (time_angle + math.pi) / (2.0 * math.pi)
    knot_index = jnp.arange(KNOTS, dtype=jnp.float32).reshape((KNOTS,) + (1,) * time_angle.ndim)
    offsets = jnp.mod(position[None] - knot_index + KNOTS / 2.0, KNOTS) - KNOTS / 2.0
    return (bspline(offsets), bspline_slope(offsets))

def conditioner_inputs(link_phase, active):
    frozen = 1.0 - active.astype(jnp.float32)
    channels = []
    for direction in range(4):
        if direction == 0:
            channels.append(jnp.cos(link_phase[direction]) * frozen)
            channels.append(jnp.sin(link_phase[direction]) * frozen)
        else:
            channels.append(jnp.cos(link_phase[direction]))
            channels.append(jnp.sin(link_phase[direction]))
    return jnp.stack(channels, axis=0)

def tap_rows(padded, block_index):
    shift_t = block_index // 9 - 1
    shift_z = block_index // 3 % 3 - 1
    shift_y = block_index % 3 - 1
    centre = region_view(padded, shift_t, shift_z, shift_y)
    return jnp.concatenate([along_rows(centre, -1), centre, along_rows(centre, 1)], axis=0)

def conv_forward(padded, kernel, bias_hidden):
    summed = None
    for block_index in range(27):
        rows_in = tap_rows(padded, block_index)
        part_sum = jnp.einsum('ci,c...->i...', kernel[24 * block_index:24 * block_index + 24], rows_in, precision=PRECISE)
        summed = part_sum if summed is None else summed + part_sum
    return summed + bias_hidden[:, None, None, None]

def coupling_forward(padded, time_angle, active_float, kernel, bias_hidden, readout, bias_out):
    hidden = jnp.tanh(conv_forward(padded, kernel, bias_hidden))
    squashed = jnp.tanh(jnp.einsum('ik,i...->k...', readout, hidden, precision=PRECISE) + bias_out[:, None, None, None])
    coeffs = SLOPE_SHARE * 2.0 * math.pi / KNOTS * squashed
    values, slopes = spline_basis(time_angle)
    moved_angle = time_angle + active_float * lax.optimization_barrier(jnp.sum(coeffs * values, axis=0))
    jacobian = 1.0 + active_float * (KNOTS / (2.0 * math.pi)) * lax.optimization_barrier(jnp.sum(coeffs * slopes, axis=0))
    return (hidden, squashed, values, slopes, moved_angle, jacobian)

def coupling_backward(padded, hidden, squashed, values, slopes, jacobian, active_float, force_field, readout, root_volume):
    ratio_const = KNOTS / (2.0 * math.pi)
    scale_const = SLOPE_SHARE * 2.0 * math.pi / KNOTS
    coeff_grad = active_float * (force_field * values - ratio_const * slopes / jacobian) / root_volume
    logit_grad = coeff_grad * scale_const * (1.0 - squashed * squashed)
    readout_part = jnp.einsum('i...,k...->ik', hidden, logit_grad, precision=PRECISE)
    out_part = lax.optimization_barrier(jnp.sum(logit_grad, axis=(1, 2, 3)))
    pre_grad = jnp.einsum('ik,k...->i...', readout, logit_grad, precision=PRECISE) * (1.0 - hidden * hidden)
    hidden_part = lax.optimization_barrier(jnp.sum(pre_grad, axis=(1, 2, 3)))
    kernel_part = jnp.concatenate([jnp.einsum('c...,i...->ci', tap_rows(padded, block_index), pre_grad, precision=PRECISE) for block_index in range(27)], axis=0)
    return (kernel_part, hidden_part, readout_part, out_part)

def time_pairing(time_angle, frame_quat, solution, solution_ahead, eta_field, eta_ahead):
    quadruple = rotate_one(frame_quat[0:4], time_angle)
    split_shape = (2, 4, 2, 2) + solution.shape[1:]
    forward = spin_apply(0, 0, colour_apply(quadruple, solution_ahead.reshape(split_shape), False))
    backward = spin_apply(1, 0, colour_apply(quadruple, solution.reshape(split_shape), True))
    kappas = jnp.asarray(KAPPAS, jnp.float32).reshape((2, 1, 1, 1, 1, 1, 1))
    return -jnp.sum(kappas * (eta_field.reshape(split_shape) * forward + eta_ahead.reshape(split_shape) * backward))

def flavour_dot(first_field, second_field):
    return lax.optimization_barrier(jnp.sum((first_field * second_field).reshape((2, -1)), axis=1))

def per_component(scalars):
    return jnp.repeat(scalars, 16).reshape((32, 1, 1, 1))

def wrap_pad(tensor, margin, antiperiodic):
    row_span = margin * X_LEN
    lower_rim = tensor[:, -margin:]
    upper_rim = tensor[:, :margin]
    if antiperiodic:
        lower_rim = -lower_rim
        upper_rim = -upper_rim
    padded = jnp.concatenate([lower_rim, tensor, upper_rim], axis=1)
    padded = jnp.concatenate([padded[:, :, -margin:], padded, padded[:, :, :margin]], axis=2)
    return jnp.concatenate([padded[..., -row_span:], padded, padded[..., :row_span]], axis=3)

def reference(pseudo, frame_quat, link_phase, active, kernel, bias_hidden, readout, bias_out):
    active_float = active.astype(jnp.float32)
    padded_inputs = wrap_pad(conditioner_inputs(link_phase, active), 1, False)
    hidden, squashed, values, slopes, moved_angle, jacobian = coupling_forward(padded_inputs, link_phase[0], active_float, kernel, bias_hidden, readout, bias_out)
    angles = jnp.concatenate([moved_angle[None], link_phase[1:]], axis=0)
    gauge_ext = wrap_pad(rotate_links(frame_quat, angles), 1, False)

    def normal_apply(spinor):
        applied = wilson(wrap_pad(spinor, 1, True), gauge_ext, False)
        return wilson(wrap_pad(applied, 1, True), gauge_ext, True)
    solution = jnp.zeros_like(pseudo)
    residual = pseudo
    direction_field = pseudo
    norm_now = flavour_dot(residual, residual)
    for iteration in range(ITERS):
        applied = normal_apply(direction_field)
        step_len = norm_now / flavour_dot(direction_field, applied)
        solution = solution + per_component(step_len) * direction_field
        residual = residual - per_component(step_len) * applied
        if iteration + 1 < ITERS:
            norm_next = flavour_dot(residual, residual)
            direction_field = residual + per_component(norm_next / norm_now) * direction_field
            norm_now = norm_next
    eta_field = wilson(wrap_pad(solution, 1, True), gauge_ext, False)
    time_sign = jnp.where(jnp.arange(NT) == NT - 1, -1.0, 1.0).astype(jnp.float32).reshape((1, NT, 1, 1))
    solution_ahead = jnp.roll(solution, -1, axis=1) * time_sign
    eta_ahead = jnp.roll(eta_field, -1, axis=1) * time_sign

    def pairing(time_angle):
        return time_pairing(time_angle, frame_quat, solution, solution_ahead, eta_field, eta_ahead)
    force_field = -2.0 * jax.grad(pairing)(moved_angle)
    root_volume = math.sqrt(NT * NZ * NY * X_LEN)
    kernel_part, hidden_part, readout_part, out_part = coupling_backward(padded_inputs, hidden, squashed, values, slopes, jacobian, active_float, force_field, readout, root_volume)
    return (solution, force_field, kernel_part, hidden_part, readout_part, out_part)
```

```python
import math

import jax
import jax.numpy as jnp
from jax import lax
from jax.experimental import pallas as pl
from jax.experimental.pallas import tpu as pltpu
from jax.sharding import PartitionSpec as P

X_LEN = 32
ITERS = 3
KNOTS = 8


PRECISE = lax.Precision.HIGHEST
KAPPAS = (0.12, 0.1)
SLOPE_SHARE = 0.5


def extended(cells, sides, width):
    for axis, dim in sides:
        count = lax.axis_size(axis)
        head = lax.slice_in_dim(cells, 0, width, axis=dim)
        tail = lax.slice_in_dim(cells, cells.shape[dim] - width, cells.shape[dim], axis=dim)
        cells = jnp.concatenate(
            [
                lax.ppermute(tail, axis, [(i, (i + 1) % count) for i in range(count)]),
                cells,
                lax.ppermute(head, axis, [((i + 1) % count, i) for i in range(count)]),
            ],
            axis=dim,
        )
    return cells


def along_rows(tensor, stride):
    positions = jnp.arange(tensor.shape[-1]) % X_LEN
    if stride > 0:
        return jnp.where(
            positions == X_LEN - 1,
            jnp.roll(tensor, X_LEN - 1, axis=-1),
            jnp.roll(tensor, -1, axis=-1),
        )
    return jnp.where(
        positions == 0, jnp.roll(tensor, 1 - X_LEN, axis=-1), jnp.roll(tensor, 1, axis=-1)
    )


def region_view(tensor, shift_t, shift_z, shift_y):
    span_t = tensor.shape[-3] - 2
    span_z = tensor.shape[-2] - 2
    span_yx = tensor.shape[-1] - 2 * X_LEN
    start_y = (1 + shift_y) * X_LEN
    return tensor[
        ...,
        1 + shift_t : 1 + shift_t + span_t,
        1 + shift_z : 1 + shift_z + span_z,
        start_y : start_y + span_yx,
    ]


def rotate_one(quadruple, theta_field):
    cosine = jnp.cos(theta_field)
    sine_part = jnp.sin(theta_field)
    return jnp.stack(
        [
            cosine * quadruple[0] - sine_part * quadruple[1],
            cosine * quadruple[1] + sine_part * quadruple[0],
            cosine * quadruple[2] - sine_part * quadruple[3],
            cosine * quadruple[3] + sine_part * quadruple[2],
        ],
        axis=0,
    )


def rotate_links(frame_quat, angles):
    return jnp.concatenate(
        [
            rotate_one(frame_quat[4 * direction : 4 * direction + 4], angles[direction])
            for direction in range(4)
        ],
        axis=0,
    )


def bspline(offsets):
    distance = jnp.abs(offsets)
    outer_part = jnp.maximum(2.0 - distance, 0.0)
    inner_part = jnp.maximum(1.0 - distance, 0.0)
    return (outer_part**3 - 4.0 * inner_part**3) / 6.0


def bspline_slope(offsets):
    distance = jnp.abs(offsets)
    outer_part = jnp.maximum(2.0 - distance, 0.0)
    inner_part = jnp.maximum(1.0 - distance, 0.0)
    return jnp.sign(offsets) * (4.0 * inner_part**2 - outer_part**2) / 2.0


def spline_basis(time_angle):
    position = KNOTS * (time_angle + math.pi) / (2.0 * math.pi)
    knot_index = jnp.arange(KNOTS, dtype=jnp.float32).reshape((KNOTS,) + (1,) * time_angle.ndim)
    offsets = jnp.mod(position[None] - knot_index + KNOTS / 2.0, KNOTS) - KNOTS / 2.0
    return (bspline(offsets), bspline_slope(offsets))


def conditioner_inputs(link_phase, active):
    frozen = 1.0 - active.astype(jnp.float32)
    channels = []
    for direction in range(4):
        if direction == 0:
            channels.append(jnp.cos(link_phase[direction]) * frozen)
            channels.append(jnp.sin(link_phase[direction]) * frozen)
        else:
            channels.append(jnp.cos(link_phase[direction]))
            channels.append(jnp.sin(link_phase[direction]))
    return jnp.stack(channels, axis=0)


def tap_rows(padded, block_index):
    shift_t = block_index // 9 - 1
    shift_z = block_index // 3 % 3 - 1
    shift_y = block_index % 3 - 1
    centre = region_view(padded, shift_t, shift_z, shift_y)
    return jnp.concatenate([along_rows(centre, -1), centre, along_rows(centre, 1)], axis=0)


def conv_forward(padded, kernel, bias_hidden):
    summed = None
    for block_index in range(27):
        rows_in = tap_rows(padded, block_index)
        part_sum = jnp.einsum(
            "ci,c...->i...",
            kernel[24 * block_index : 24 * block_index + 24],
            rows_in,
            precision=PRECISE,
        )
        summed = part_sum if summed is None else summed + part_sum
    return summed + bias_hidden[:, None, None, None]


def coupling_forward(padded, time_angle, active_float, kernel, bias_hidden, readout, bias_out):
    hidden = jnp.tanh(conv_forward(padded, kernel, bias_hidden))
    squashed = jnp.tanh(
        jnp.einsum("ik,i...->k...", readout, hidden, precision=PRECISE)
        + bias_out[:, None, None, None]
    )
    coeffs = SLOPE_SHARE * 2.0 * math.pi / KNOTS * squashed
    values, slopes = spline_basis(time_angle)
    moved_angle = time_angle + active_float * jnp.sum(coeffs * values, axis=0)
    jacobian = 1.0 + active_float * (KNOTS / (2.0 * math.pi)) * jnp.sum(coeffs * slopes, axis=0)
    return (hidden, squashed, values, slopes, moved_angle, jacobian)


def coupling_backward(
    padded,
    hidden,
    squashed,
    values,
    slopes,
    jacobian,
    active_float,
    force_field,
    readout,
    root_volume,
):
    ratio_const = KNOTS / (2.0 * math.pi)
    scale_const = SLOPE_SHARE * 2.0 * math.pi / KNOTS
    coeff_grad = (
        active_float * (force_field * values - ratio_const * slopes / jacobian) / root_volume
    )
    logit_grad = coeff_grad * scale_const * (1.0 - squashed * squashed)
    readout_part = jnp.einsum("i...,k...->ik", hidden, logit_grad, precision=PRECISE)
    out_part = jnp.sum(logit_grad, axis=(1, 2, 3))
    pre_grad = jnp.einsum("ik,k...->i...", readout, logit_grad, precision=PRECISE) * (
        1.0 - hidden * hidden
    )
    hidden_part = jnp.sum(pre_grad, axis=(1, 2, 3))
    kernel_part = jnp.concatenate(
        [
            jnp.einsum("c...,i...->ci", tap_rows(padded, block_index), pre_grad, precision=PRECISE)
            for block_index in range(27)
        ],
        axis=0,
    )
    return (kernel_part, hidden_part, readout_part, out_part)


GROUP = ("ta", "gz", "gy")
MESH = pl.DeviceIdType.MESH
F32 = jnp.float32

SPIN_K = {
    1: [[(-1, 0, 1), (1, 0, 0)], [(1, 1, 1), (-1, 1, 0)]],
    2: [[(1, 1, 0), (1, 1, 1)], [(-1, 0, 0), (-1, 0, 1)]],
    3: [[(-1, 1, 1), (1, 1, 0)], [(-1, 0, 1), (1, 0, 0)]],
}
TURN = {0: [[(-1, 0, 0), (-1, 0, 1)], [(-1, 1, 0), (-1, 1, 1)]], **SPIN_K}
BACK = {0: [[(1, 0, 0), (1, 0, 1)], [(1, 1, 0), (1, 1, 1)]], **SPIN_K}


def group_size():
    return lax.axis_size("ta") * lax.axis_size("gz") * lax.axis_size("gy")


def each(count, step):
    if count <= 16:
        for index in range(count):
            step(index)
    else:

        def looped(index, carry):
            step(index)
            return carry

        lax.fori_loop(0, count, looped, 0)


def peer(offset):
    nz, ny = lax.axis_size("gz"), lax.axis_size("gy")
    mine = (lax.axis_index("ta") * nz + lax.axis_index("gz")) * ny + lax.axis_index("gy")
    target = lax.rem(mine + offset, group_size())
    return {
        "groups": lax.axis_index("groups"),
        "ta": target // (nz * ny),
        "gz": lax.rem(target // ny, nz),
        "gy": lax.rem(target, ny),
    }


def greet_group():
    barrier = pltpu.get_barrier_semaphore()
    count = group_size() - 1

    def greet(index):
        pl.semaphore_signal(barrier, inc=1, device_id=peer(index + 1), device_id_type=MESH)

    each(count, greet)
    pl.semaphore_wait(barrier, count)


def step_along(axis, distance):
    count = lax.axis_size(axis)
    return {axis: lax.rem(lax.axis_index(axis) + (distance + count), count)}


def rows_of(shape):
    return lax.broadcasted_iota(jnp.int32, shape, len(shape) - 2)


def lanes_of(shape):
    return lax.broadcasted_iota(jnp.int32, shape, len(shape) - 1)


def turned(tensor, shift, axis):
    size = tensor.shape[axis]
    shift = shift % size
    return tensor if shift == 0 else pltpu.roll(tensor, shift, axis)


def colour_forward(quad, half):
    a_re, a_im, b_re, b_im = quad
    result = []
    for spin in range(2):
        (u_re, u_im), (l_re, l_im) = half[spin]
        result.append(
            [
                [
                    a_re * u_re - a_im * u_im + b_re * l_re - b_im * l_im,
                    a_re * u_im + a_im * u_re + b_re * l_im + b_im * l_re,
                ],
                [
                    a_re * l_re + a_im * l_im - b_re * u_re - b_im * u_im,
                    a_re * l_im - a_im * l_re - b_re * u_im + b_im * u_re,
                ],
            ]
        )
    return result


def colour_adjoint(quad, half):
    a_re, a_im, b_re, b_im = quad
    result = []
    for spin in range(2):
        (u_re, u_im), (l_re, l_im) = half[spin]
        result.append(
            [
                [
                    a_re * u_re + a_im * u_im - b_re * l_re + b_im * l_im,
                    a_re * u_im - a_im * u_re - b_re * l_im - b_im * l_re,
                ],
                [
                    b_re * u_re + b_im * u_im + a_re * l_re - a_im * l_im,
                    b_re * u_im - b_im * u_re + a_re * l_im + a_im * l_re,
                ],
            ]
        )
    return result


def project(field, mu, sign):
    half = []
    for spin in range(2):
        colours = []
        for colour in range(2):
            parts = []
            for part in range(2):
                flip, s, r = TURN[mu][spin][part]
                upper, lower = field[spin, colour, part], field[2 + s, colour, r]
                parts.append(upper + lower if flip * sign > 0 else upper - lower)
            colours.append(parts)
        half.append(colours)
    return half


def along_x(tensor, stride):
    place = lax.rem(lanes_of(tensor.shape), X_LEN)
    if stride > 0:
        return jnp.where(place == X_LEN - 1, turned(tensor, X_LEN - 1, 2), turned(tensor, -1, 2))
    return jnp.where(place == 0, turned(tensor, 1 - X_LEN, 2), turned(tensor, 1, 2))


def each_part():
    return [(s, c, r) for s in range(2) for c in range(2) for r in range(2)]


def cg_kernel(
    pseudo_ref,
    gauge_ref,
    sol_ref,
    force_ref,
    links,
    bank,
    dvec,
    xs,
    es,
    out,
    hop,
    t_send,
    t_recv,
    z_send,
    z_recv,
    y_send,
    y_recv,
    f_send,
    f_recv,
    ratio,
    red_send,
    red_recv,
    halo_ssem,
    halo_rsem,
    f_ssem,
    f_rsem,
    red_ssem,
    red_rsem,
):
    nt, nz, width = pseudo_ref.shape[-3:]
    shape = (2, nt * nz, width)
    others = group_size() - 1
    row, lane = rows_of(shape), lanes_of(shape)
    z_place = lax.rem(row, nz)
    t_low = row < (nt - 1) * nz
    y_count = width // X_LEN
    kappa = jnp.where(lax.broadcasted_iota(jnp.int32, shape, 0) == 0, KAPPAS[0], KAPPAS[1]).astype(F32)
    last_sign = jnp.where(lax.axis_index("ta") == lax.axis_size("ta") - 1, -1.0, 1.0).astype(F32)
    first_sign = jnp.where(lax.axis_index("ta") == 0, -1.0, 1.0).astype(F32)

    for mu in range(4):
        for part in range(4):
            for t in range(nt):
                links[mu, part, t * nz : (t + 1) * nz] = gauge_ref[mu, part, t]
    for flavour in range(2):
        for s in range(4):
            for c in range(2):
                for r in range(2):
                    for t in range(nt):
                        rows = slice(t * nz, (t + 1) * nz)
                        bank[0, s, c, r, flavour, rows] = pseudo_ref[flavour, s, c, r, t]
    for s in range(4):
        zero = jnp.zeros((2, 2) + shape, F32)
        bank[1, s] = zero
        dvec[s] = zero
        xs[s] = zero
        es[s] = zero
        out[s] = zero
    ratio[...] = jnp.ones(ratio.shape, F32)

    greet_group()

    def reduce_copy(parity, index):
        return pltpu.make_async_remote_copy(
            src_ref=red_send.at[parity],
            dst_ref=red_recv.at[parity, index],
            send_sem=red_ssem.at[parity, index],
            recv_sem=red_rsem.at[parity, index],
            device_id=peer(index + 1),
            device_id_type=MESH,
        )

    def start_sum(parity, total):
        folded = total[:, :, 0:128]
        for start in range(128, width, 128):
            folded = folded + total[:, :, start : start + 128]
        sums = jnp.sum(folded, axis=1, keepdims=True)
        tile_row = rows_of((8, 128))
        red_send[parity] = jnp.where(tile_row == 0, sums[0], jnp.where(tile_row == 1, sums[1], 0.0))
        each(others, lambda index: reduce_copy(parity, index).start())

    def finish_sum(parity):
        each(others, lambda index: reduce_copy(parity, index).wait())
        total = red_send[parity] + jnp.sum(red_recv[parity], axis=0)
        total = jnp.broadcast_to(jnp.sum(total, axis=1, keepdims=True), (8, 128))
        return jnp.where(rows_of((8, 128)) < 2, total, 1.0)

    def spread(pair):
        return jnp.stack([jnp.broadcast_to(pair[f : f + 1, 0:1], shape[1:]) for f in range(2)])

    def halo_copy(side, parity):
        send, recv, axis = ((t_send, t_recv, "ta"), (z_send, z_recv, "gz"), (y_send, y_recv, "gy"))[side // 2]
        return pltpu.make_async_remote_copy(
            src_ref=send.at[side % 2],
            dst_ref=recv.at[parity, side % 2],
            send_sem=halo_ssem.at[side],
            recv_sem=halo_rsem.at[parity, side],
            device_id=step_along(axis, -1 if side % 2 == 0 else 1),
            device_id_type=MESH,
        )

    def pack_t(half, ahead, send):
        for s, c in ((0, 0), (0, 1), (1, 0), (1, 1)):
            first, second = half[s][c]
            moved = [turned(v, -nz if ahead else nz, 1) for v in (first, second)]
            if ahead:
                send[2 * s + c] = jnp.where(row < nz, second, moved[0]) if nt == 2 else None
            else:
                send[2 * s + c] = jnp.where(row < nz, moved[0], second)
            yield s, c, moved

    def place_t(halo, moved, ahead, part):
        if ahead:
            edge = halo if part == 0 else turned(halo, nz, 1)
            return jnp.where(t_low, moved, edge)
        edge = halo if part == 0 else turned(halo, nz, 1)
        return jnp.where(row < nz, edge, moved)

    def send_halos(field, parity):
        for mu in range(3):
            for back in range(2):
                half = project(field, mu, -1 if back else 1)
                if back:
                    half = colour_adjoint([links[mu, p] for p in range(4)], half)
                side = 2 * mu + back
                if mu == 0:
                    for s, c, moved in pack_t(half, not back, t_send.at[back]):
                        for r in range(2):
                            hop[side, s, c, r] = moved[r]
                elif mu == 1:
                    packed = [None, None]
                    for s, c, r in each_part():
                        value = half[s][c][r]
                        hop[side, s, c, r] = turned(value, 1 if back else -1, 1)
                        slot = 2 * s + c
                        put = turned(value, slot - (nz - 1) if back else slot, 1)
                        packed[r] = put if packed[r] is None else jnp.where(z_place == slot, put, packed[r])
                    for r in range(2):
                        z_send[back, r] = packed[r]
                else:
                    packed = None
                    for s, c, r in each_part():
                        value = half[s][c][r]
                        hop[side, s, c, r] = turned(value, X_LEN if back else -X_LEN, 2)
                        slot = 4 * s + 2 * c + r
                        put = turned(value, (slot - (y_count - 1) if back else slot) * X_LEN, 2)
                        packed = put if packed is None else jnp.where(lane // X_LEN == slot, put, packed)
                    y_send[back] = packed
                halo_copy(side, parity).start()

    def add_hop(total, half, mu, back):
        sign = 1 if back else -1
        for s, c, r in each_part():
            flip, source, part = BACK[mu][s][r]
            top, low = half[s][c][r], half[source][c][part]
            if total[s][c][r] is None:
                total[s][c][r] = top
                total[2 + s][c][r] = low if flip * sign > 0 else -low
            else:
                total[s][c][r] = total[s][c][r] + top
                lower = total[2 + s][c][r]
                total[2 + s][c][r] = lower + low if flip * sign > 0 else lower - low

    def turned_wilson(source, parity):
        field = {
            (s, c, r): bank[source, s, c, r] for s in range(4) for c in range(2) for r in range(2)
        }
        send_halos(field, parity)
        total = [[[None, None], [None, None]] for _ in range(4)]
        quad = [links[3, p] for p in range(4)]
        half = project(field, 3, 1)
        ahead = [[[along_x(half[s][c][r], 1) for r in range(2)] for c in range(2)] for s in range(2)]
        add_hop(total, colour_forward(quad, ahead), 3, False)
        half = colour_adjoint(quad, project(field, 3, -1))
        behind = [[[along_x(half[s][c][r], -1) for r in range(2)] for c in range(2)] for s in range(2)]
        add_hop(total, behind, 3, True)
        for s in range(4):
            for c in range(2):
                for r in range(2):
                    out[s, c, r] = total[s][c][r]
        for mu in (2, 1, 0):
            total = [[[out[s, c, r] for r in range(2)] for c in range(2)] for s in range(4)]
            for back in range(2):
                side = 2 * mu + back
                halo_copy(side, parity).wait()
                half = [[[None, None], [None, None]] for _ in range(2)]
                for s, c, r in each_part():
                    moved = hop[side, s, c, r]
                    if mu == 0:
                        halo = t_recv[parity, back, 2 * s + c] * (first_sign if back else last_sign)
                        merged = place_t(halo, moved, not back, r)
                    elif mu == 1:
                        slot = 2 * s + c
                        halo = z_recv[parity, back, r]
                        if back:
                            merged = jnp.where(z_place == 0, turned(halo, -slot, 1), moved)
                        else:
                            merged = jnp.where(z_place == nz - 1, turned(halo, nz - 1 - slot, 1), moved)
                    else:
                        slot = 4 * s + 2 * c + r
                        halo = y_recv[parity, back]
                        if back:
                            merged = jnp.where(lane < X_LEN, turned(halo, -slot * X_LEN, 2), moved)
                        else:
                            placed = turned(halo, (y_count - 1 - slot) * X_LEN, 2)
                            merged = jnp.where(lane >= width - X_LEN, placed, moved)
                    half[s][c][r] = merged
                if not back:
                    half = colour_forward([links[mu, p] for p in range(4)], half)
                add_hop(total, half, mu, back)
            for s in range(4):
                for c in range(2):
                    for r in range(2):
                        value = total[s][c][r]
                        if mu == 0:
                            value = bank[source, s, c, r] - kappa * value
                            value = value if s < 2 else -value
                        out[s, c, r] = value

    def iteration(k, carry):
        start_sum(0, sum(jnp.sum(bank[0, s] * bank[0, s], axis=(0, 1)) for s in range(4)))
        turned_wilson(0, 0)
        norm = finish_sum(0)
        growth = spread(jnp.where(k > 0, norm / ratio[...], 0.0))
        ratio[...] = norm
        square = jnp.zeros(shape, F32)
        for s in range(4):
            image = out[s] + growth * bank[1, s]
            bank[1, s] = image
            dvec[s] = bank[0, s] + growth * dvec[s]
            square = square + jnp.sum(image * image, axis=(0, 1))
        start_sum(1, square)

        @pl.when(k < ITERS - 1)
        def _():
            turned_wilson(1, 1)

        length = spread(ratio[...] / finish_sum(1))
        for s in range(4):
            xs[s] = xs[s] + length * dvec[s]
            es[s] = es[s] + length * bank[1, s]
            bank[0, s] = bank[0, s] - length * out[s]
        return carry

    lax.fori_loop(0, ITERS, iteration, 0)

    def front_copy(which):
        return pltpu.make_async_remote_copy(
            src_ref=f_send.at[which],
            dst_ref=f_recv.at[which],
            send_sem=f_ssem.at[which],
            recv_sem=f_rsem.at[which],
            device_id=step_along("ta", -1),
            device_id_type=MESH,
        )

    for which, held in enumerate((xs, es)):
        half = project({(s, c, r): held[s, c, r] for s in range(4) for c in range(2) for r in range(2)}, 0, 1)
        for s, c, moved in pack_t(half, True, f_send.at[which]):
            for r in range(2):
                hop[which, s, c, r] = moved[r]
        front_copy(which).start()
    for flavour in range(2):
        for s in range(4):
            for c in range(2):
                for r in range(2):
                    for t in range(nt):
                        sol_ref[flavour, s, c, r, t] = xs[s, c, r, flavour, t * nz : (t + 1) * nz]
    force = jnp.zeros(shape, F32)
    for which, held in enumerate((es, xs)):
        front_copy(which).wait()
        half = [[[None, None], [None, None]] for _ in range(2)]
        for s, c, r in each_part():
            half[s][c][r] = place_t(f_recv[which, 2 * s + c] * last_sign, hop[which, s, c, r], True, r)
        image = colour_forward([links[0, p] for p in range(4)], half)
        for s in range(2):
            for c in range(2):
                left = [held[s, c, r] + held[2 + s, c, r] for r in range(2)]
                term = left[1] * image[s][c][0] - left[0] * image[s][c][1]
                force = force + term if c == 0 else force - term
    force = force * (2.0 * kappa)
    force = force[0] + force[1]
    for t in range(nt):
        force_ref[t] = force[t * nz : (t + 1) * nz]


def conjugate_gradient(pseudo, gauge):
    nt, nz, width = pseudo.shape[1:]
    rows = nt * nz
    others = group_size() - 1
    field = (4, 2, 2, 2, rows, width)
    vmem = lambda *dims: pltpu.VMEM(dims, F32)
    dma = lambda *dims: pltpu.SemaphoreType.DMA(dims)
    sol, force = pl.pallas_call(
        cg_kernel,
        out_shape=(
            jax.ShapeDtypeStruct((2, 4, 2, 2, nt, nz, width), F32),
            jax.ShapeDtypeStruct((nt, nz, width), F32),
        ),
        in_specs=[pl.BlockSpec(memory_space=pltpu.VMEM)] * 2,
        out_specs=[pl.BlockSpec(memory_space=pltpu.VMEM)] * 2,
        scratch_shapes=[
            vmem(4, 4, rows, width),
            vmem(2, *field),
            vmem(*field),
            vmem(*field),
            vmem(*field),
            vmem(*field),
            vmem(6, 2, 2, 2, 2, rows, width),
            vmem(2, 4, 2, rows, width),
            vmem(2, 2, 4, 2, rows, width),
            vmem(2, 2, 2, rows, width),
            vmem(2, 2, 2, 2, rows, width),
            vmem(2, 2, rows, width),
            vmem(2, 2, 2, rows, width),
            vmem(2, 4, 2, rows, width),
            vmem(2, 4, 2, rows, width),
            vmem(8, 128),
            vmem(2, 8, 128),
            vmem(2, others, 8, 128),
            dma(6),
            dma(2, 6),
            dma(2),
            dma(2),
            dma(2, others),
            dma(2, others),
        ],
        compiler_params=pltpu.CompilerParams(
            collective_id=0, has_side_effects=True, vmem_limit_bytes=32 * 1024 * 1024
        ),
    )(pseudo.reshape((2, 4, 2, 2, nt, nz, width)), gauge.reshape((4, 4, nt, nz, width)))
    return sol.reshape(pseudo.shape), force


def sum_kernel(data_ref, out_ref, landed, reduced, ssem, rsem, gather_ssem, gather_rsem):
    count = group_size()
    chunk = data_ref.shape[0] // count
    nz, ny = lax.axis_size("gz"), lax.axis_size("gy")
    mine = (lax.axis_index("ta") * nz + lax.axis_index("gz")) * ny + lax.axis_index("gy")
    greet_group()

    def part_of(device):
        return pl.ds(pl.multiple_of(device * chunk, 8), chunk)

    def scatter(index):
        return pltpu.make_async_remote_copy(
            src_ref=data_ref.at[part_of(lax.rem(mine + index + 1, count))],
            dst_ref=landed.at[index],
            send_sem=ssem.at[index],
            recv_sem=rsem.at[index],
            device_id=peer(index + 1),
            device_id_type=MESH,
        )

    def gather(index, owner):
        return pltpu.make_async_remote_copy(
            src_ref=reduced,
            dst_ref=out_ref.at[part_of(owner)],
            send_sem=gather_ssem.at[index],
            recv_sem=gather_rsem.at[index],
            device_id=peer(index + 1),
            device_id_type=MESH,
        )

    each(count - 1, lambda index: scatter(index).start())
    each(count - 1, lambda index: scatter(index).wait())
    total = data_ref[part_of(mine)] + jnp.sum(landed[...], axis=0)
    reduced[...] = total
    each(count - 1, lambda index: gather(index, mine).start())
    out_ref[part_of(mine)] = total
    each(count - 1, lambda index: gather(index, lax.rem(mine + count - index - 1, count)).wait())


def group_sum(arrays):
    count = group_size()
    flat = jnp.concatenate([a.reshape(-1) for a in arrays])
    chunk = -(-flat.size // (count * 1024)) * 8
    data = jnp.pad(flat, (0, count * chunk * 128 - flat.size)).reshape((count * chunk, 128))
    dma = lambda *dims: pltpu.SemaphoreType.DMA(dims)
    summed = pl.pallas_call(
        sum_kernel,
        out_shape=jax.ShapeDtypeStruct(data.shape, F32),
        in_specs=[pl.BlockSpec(memory_space=pltpu.VMEM)],
        out_specs=pl.BlockSpec(memory_space=pltpu.VMEM),
        scratch_shapes=[
            pltpu.VMEM((count - 1, chunk, 128), F32),
            pltpu.VMEM((chunk, 128), F32),
            dma(count - 1),
            dma(count - 1),
            dma(count - 1),
            dma(count - 1),
        ],
        compiler_params=pltpu.CompilerParams(
            collective_id=1, has_side_effects=True, vmem_limit_bytes=32 * 1024 * 1024
        ),
    )(data).reshape(-1)
    results, start = [], 0
    for a in arrays:
        results.append(summed[start : start + a.size].reshape(a.shape))
        start += a.size
    return results


def extend(tensor, margin):
    face_ext = extended(tensor, (("ta", 1), ("gz", 2)), margin)
    return extended(face_ext, (("gy", 3),), margin * X_LEN)


def on_device(pseudo, frame_quat, link_phase, active, kernel, bias_hidden, readout, bias_out):
    active_float = active.astype(jnp.float32)
    padded_inputs = extend(conditioner_inputs(link_phase, active), 1)
    hidden, squashed, values, slopes, moved_angle, jacobian = coupling_forward(
        padded_inputs, link_phase[0], active_float, kernel, bias_hidden, readout, bias_out
    )
    angles = jnp.concatenate([moved_angle[None], link_phase[1:]], axis=0)
    gauge_core = rotate_links(frame_quat, angles)
    solution, force_field = conjugate_gradient(pseudo, gauge_core)
    root_volume = math.sqrt(active.size * group_size())
    kernel_part, hidden_part, readout_part, out_part = coupling_backward(
        padded_inputs,
        hidden,
        squashed,
        values,
        slopes,
        jacobian,
        active_float,
        force_field,
        readout,
        root_volume,
    )
    grad_kernel, grad_hidden, grad_readout, grad_out = group_sum(
        (kernel_part, hidden_part, readout_part, out_part)
    )
    return (solution, force_field, grad_kernel, grad_hidden, grad_readout, grad_out)


def solution(mesh):
    return jax.shard_map(
        on_device,
        mesh=mesh,
        in_specs=(
            P("groups", "ta", "gz", "gy"),
            P("groups", "ta", "gz", "gy"),
            P("groups", "ta", "gz", "gy"),
            P(("groups", "ta"), "gz", "gy"),
            P(),
            P(),
            P(),
            P(),
        ),
        out_specs=(
            P("groups", "ta", "gz", "gy"),
            P(("groups", "ta"), "gz", "gy"),
            P("groups", None),
            P("groups"),
            P("groups", None),
            P("groups"),
        ),
        check_vma=False,
    )
```

```python
import math

import jax
import jax.numpy as jnp
from jax import lax
from jax.experimental import pallas as pl
from jax.experimental.pallas import tpu as pltpu
from jax.sharding import PartitionSpec as P

X_LEN = 32
ITERS = 3
KNOTS = 8


PRECISE = lax.Precision.HIGHEST
KAPPAS = (0.12, 0.1)
SLOPE_SHARE = 0.5


def rotate_one(quadruple, theta_field):
    cosine = jnp.cos(theta_field)
    sine_part = jnp.sin(theta_field)
    return jnp.stack(
        [
            cosine * quadruple[0] - sine_part * quadruple[1],
            cosine * quadruple[1] + sine_part * quadruple[0],
            cosine * quadruple[2] - sine_part * quadruple[3],
            cosine * quadruple[3] + sine_part * quadruple[2],
        ],
        axis=0,
    )


def rotate_links(frame_quat, angles):
    return jnp.concatenate(
        [
            rotate_one(frame_quat[4 * direction : 4 * direction + 4], angles[direction])
            for direction in range(4)
        ],
        axis=0,
    )


def bspline(offsets):
    distance = jnp.abs(offsets)
    outer_part = jnp.maximum(2.0 - distance, 0.0)
    inner_part = jnp.maximum(1.0 - distance, 0.0)
    return (outer_part**3 - 4.0 * inner_part**3) / 6.0


def bspline_slope(offsets):
    distance = jnp.abs(offsets)
    outer_part = jnp.maximum(2.0 - distance, 0.0)
    inner_part = jnp.maximum(1.0 - distance, 0.0)
    return jnp.sign(offsets) * (4.0 * inner_part**2 - outer_part**2) / 2.0


def spline_basis(time_angle):
    position = KNOTS * (time_angle + math.pi) / (2.0 * math.pi)
    knot_index = jnp.arange(KNOTS, dtype=jnp.float32).reshape((KNOTS,) + (1,) * time_angle.ndim)
    offsets = jnp.mod(position[None] - knot_index + KNOTS / 2.0, KNOTS) - KNOTS / 2.0
    return (bspline(offsets), bspline_slope(offsets))


def conditioner_inputs(link_phase, active):
    frozen = 1.0 - active.astype(jnp.float32)
    channels = []
    for direction in range(4):
        if direction == 0:
            channels.append(jnp.cos(link_phase[direction]) * frozen)
            channels.append(jnp.sin(link_phase[direction]) * frozen)
        else:
            channels.append(jnp.cos(link_phase[direction]))
            channels.append(jnp.sin(link_phase[direction]))
    return jnp.stack(channels, axis=0)


GROUP = ("ta", "gz", "gy")
MESH = pl.DeviceIdType.MESH
F32 = jnp.float32

SPIN_K = {
    1: [[(-1, 0, 1), (1, 0, 0)], [(1, 1, 1), (-1, 1, 0)]],
    2: [[(1, 1, 0), (1, 1, 1)], [(-1, 0, 0), (-1, 0, 1)]],
    3: [[(-1, 1, 1), (1, 1, 0)], [(-1, 0, 1), (1, 0, 0)]],
}
TURN = {0: [[(-1, 0, 0), (-1, 0, 1)], [(-1, 1, 0), (-1, 1, 1)]], **SPIN_K}
BACK = {0: [[(1, 0, 0), (1, 0, 1)], [(1, 1, 0), (1, 1, 1)]], **SPIN_K}


def group_size():
    return lax.axis_size("ta") * lax.axis_size("gz") * lax.axis_size("gy")


def each(count, step):
    if count <= 16:
        for index in range(count):
            step(index)
    else:

        def looped(index, carry):
            step(index)
            return carry

        lax.fori_loop(0, count, looped, 0)


def peer(offset):
    nz, ny = lax.axis_size("gz"), lax.axis_size("gy")
    mine = (lax.axis_index("ta") * nz + lax.axis_index("gz")) * ny + lax.axis_index("gy")
    target = lax.rem(mine + offset, group_size())
    return {
        "groups": lax.axis_index("groups"),
        "ta": target // (nz * ny),
        "gz": lax.rem(target // ny, nz),
        "gy": lax.rem(target, ny),
    }


def greet_group():
    barrier = pltpu.get_barrier_semaphore()
    count = group_size() - 1

    def greet(index):
        pl.semaphore_signal(barrier, inc=1, device_id=peer(index + 1), device_id_type=MESH)

    each(count, greet)
    pl.semaphore_wait(barrier, count)


def step_along(axis, distance):
    count = lax.axis_size(axis)
    return {axis: lax.rem(lax.axis_index(axis) + (distance + count), count)}


def rows_of(shape):
    return lax.broadcasted_iota(jnp.int32, shape, len(shape) - 2)


def lanes_of(shape):
    return lax.broadcasted_iota(jnp.int32, shape, len(shape) - 1)


def turned(tensor, shift, axis):
    size = tensor.shape[axis]
    shift = shift % size
    return tensor if shift == 0 else pltpu.roll(tensor, shift, axis)


def colour_forward(quad, half):
    a_re, a_im, b_re, b_im = quad
    result = []
    for spin in range(2):
        (u_re, u_im), (l_re, l_im) = half[spin]
        result.append(
            [
                [
                    a_re * u_re - a_im * u_im + b_re * l_re - b_im * l_im,
                    a_re * u_im + a_im * u_re + b_re * l_im + b_im * l_re,
                ],
                [
                    a_re * l_re + a_im * l_im - b_re * u_re - b_im * u_im,
                    a_re * l_im - a_im * l_re - b_re * u_im + b_im * u_re,
                ],
            ]
        )
    return result


def colour_adjoint(quad, half):
    a_re, a_im, b_re, b_im = quad
    result = []
    for spin in range(2):
        (u_re, u_im), (l_re, l_im) = half[spin]
        result.append(
            [
                [
                    a_re * u_re + a_im * u_im - b_re * l_re + b_im * l_im,
                    a_re * u_im - a_im * u_re - b_re * l_im - b_im * l_re,
                ],
                [
                    b_re * u_re + b_im * u_im + a_re * l_re - a_im * l_im,
                    b_re * u_im - b_im * u_re + a_re * l_im + a_im * l_re,
                ],
            ]
        )
    return result


def project(field, mu, sign):
    half = []
    for spin in range(2):
        colours = []
        for colour in range(2):
            parts = []
            for part in range(2):
                flip, s, r = TURN[mu][spin][part]
                upper, lower = field[spin, colour, part], field[2 + s, colour, r]
                parts.append(upper + lower if flip * sign > 0 else upper - lower)
            colours.append(parts)
        half.append(colours)
    return half


def along_x(tensor, stride):
    axis = tensor.ndim - 1
    place = lax.rem(lanes_of(tensor.shape), X_LEN)
    wrap = X_LEN - 1
    if stride > 0:
        return jnp.where(place == wrap, turned(tensor, wrap, axis), turned(tensor, -1, axis))
    return jnp.where(place == 0, turned(tensor, -wrap, axis), turned(tensor, 1, axis))


def each_part():
    return [(s, c, r) for s in range(2) for c in range(2) for r in range(2)]


def cg_kernel(
    pseudo_ref,
    gauge_ref,
    sol_ref,
    force_ref,
    links,
    bank,
    dvec,
    xs,
    es,
    out,
    hop,
    t_send,
    t_recv,
    z_send,
    z_recv,
    y_send,
    y_recv,
    f_send,
    f_recv,
    ratio,
    red_send,
    red_recv,
    halo_ssem,
    halo_rsem,
    f_ssem,
    f_rsem,
    red_ssem,
    red_rsem,
):
    nt, nz, width = pseudo_ref.shape[-3:]
    shape = (2, nt * nz, width)
    others = group_size() - 1
    row, lane = rows_of(shape), lanes_of(shape)
    z_place = lax.rem(row, nz)
    t_low = row < (nt - 1) * nz
    y_count = width // X_LEN
    kappa = jnp.where(lax.broadcasted_iota(jnp.int32, shape, 0) == 0, KAPPAS[0], KAPPAS[1]).astype(F32)
    last_sign = jnp.where(lax.axis_index("ta") == lax.axis_size("ta") - 1, -1.0, 1.0).astype(F32)
    first_sign = jnp.where(lax.axis_index("ta") == 0, -1.0, 1.0).astype(F32)

    for mu in range(4):
        for part in range(4):
            for t in range(nt):
                links[mu, part, t * nz : (t + 1) * nz] = gauge_ref[mu, part, t]
    for flavour in range(2):
        for s in range(4):
            for c in range(2):
                for r in range(2):
                    for t in range(nt):
                        rows = slice(t * nz, (t + 1) * nz)
                        bank[0, s, c, r, flavour, rows] = pseudo_ref[flavour, s, c, r, t]
    for s in range(4):
        zero = jnp.zeros((2, 2) + shape, F32)
        bank[1, s] = zero
        dvec[s] = zero
        xs[s] = zero
        es[s] = zero
        out[s] = zero
    ratio[...] = jnp.ones(ratio.shape, F32)

    greet_group()

    def reduce_copy(parity, index):
        return pltpu.make_async_remote_copy(
            src_ref=red_send.at[parity],
            dst_ref=red_recv.at[parity, index],
            send_sem=red_ssem.at[parity, index],
            recv_sem=red_rsem.at[parity, index],
            device_id=peer(index + 1),
            device_id_type=MESH,
        )

    def start_sum(parity, total):
        folded = total[:, :, 0:128]
        for start in range(128, width, 128):
            folded = folded + total[:, :, start : start + 128]
        sums = jnp.sum(folded, axis=1, keepdims=True)
        tile_row = rows_of((8, 128))
        red_send[parity] = jnp.where(tile_row == 0, sums[0], jnp.where(tile_row == 1, sums[1], 0.0))
        each(others, lambda index: reduce_copy(parity, index).start())

    def finish_sum(parity):
        each(others, lambda index: reduce_copy(parity, index).wait())
        total = red_send[parity] + jnp.sum(red_recv[parity], axis=0)
        total = jnp.broadcast_to(jnp.sum(total, axis=1, keepdims=True), (8, 128))
        return jnp.where(rows_of((8, 128)) < 2, total, 1.0)

    def spread(pair):
        return jnp.stack([jnp.broadcast_to(pair[f : f + 1, 0:1], shape[1:]) for f in range(2)])

    def halo_copy(side, parity):
        send, recv, axis = ((t_send, t_recv, "ta"), (z_send, z_recv, "gz"), (y_send, y_recv, "gy"))[side // 2]
        return pltpu.make_async_remote_copy(
            src_ref=send.at[side % 2],
            dst_ref=recv.at[parity, side % 2],
            send_sem=halo_ssem.at[side],
            recv_sem=halo_rsem.at[parity, side],
            device_id=step_along(axis, -1 if side % 2 == 0 else 1),
            device_id_type=MESH,
        )

    def pack_t(half, ahead, send):
        for s, c in ((0, 0), (0, 1), (1, 0), (1, 1)):
            first, second = half[s][c]
            moved = [turned(v, -nz if ahead else nz, 1) for v in (first, second)]
            if ahead:
                send[2 * s + c] = jnp.where(row < nz, second, moved[0]) if nt == 2 else None
            else:
                send[2 * s + c] = jnp.where(row < nz, moved[0], second)
            yield s, c, moved

    def place_t(halo, moved, ahead, part):
        if ahead:
            edge = halo if part == 0 else turned(halo, nz, 1)
            return jnp.where(t_low, moved, edge)
        edge = halo if part == 0 else turned(halo, nz, 1)
        return jnp.where(row < nz, edge, moved)

    def send_halos(field, parity):
        for mu in range(3):
            for back in range(2):
                half = project(field, mu, -1 if back else 1)
                if back:
                    half = colour_adjoint([links[mu, p] for p in range(4)], half)
                side = 2 * mu + back
                if mu == 0:
                    for s, c, moved in pack_t(half, not back, t_send.at[back]):
                        for r in range(2):
                            hop[side, s, c, r] = moved[r]
                elif mu == 1:
                    packed = [None, None]
                    for s, c, r in each_part():
                        value = half[s][c][r]
                        hop[side, s, c, r] = turned(value, 1 if back else -1, 1)
                        slot = 2 * s + c
                        put = turned(value, slot - (nz - 1) if back else slot, 1)
                        packed[r] = put if packed[r] is None else jnp.where(z_place == slot, put, packed[r])
                    for r in range(2):
                        z_send[back, r] = packed[r]
                else:
                    packed = None
                    for s, c, r in each_part():
                        value = half[s][c][r]
                        hop[side, s, c, r] = turned(value, X_LEN if back else -X_LEN, 2)
                        slot = 4 * s + 2 * c + r
                        put = turned(value, (slot - (y_count - 1) if back else slot) * X_LEN, 2)
                        packed = put if packed is None else jnp.where(lane // X_LEN == slot, put, packed)
                    y_send[back] = packed
                halo_copy(side, parity).start()

    def add_hop(total, half, mu, back):
        sign = 1 if back else -1
        for s, c, r in each_part():
            flip, source, part = BACK[mu][s][r]
            top, low = half[s][c][r], half[source][c][part]
            if total[s][c][r] is None:
                total[s][c][r] = top
                total[2 + s][c][r] = low if flip * sign > 0 else -low
            else:
                total[s][c][r] = total[s][c][r] + top
                lower = total[2 + s][c][r]
                total[2 + s][c][r] = lower + low if flip * sign > 0 else lower - low

    def turned_wilson(source, parity):
        field = {
            (s, c, r): bank[source, s, c, r] for s in range(4) for c in range(2) for r in range(2)
        }
        send_halos(field, parity)
        total = [[[None, None], [None, None]] for _ in range(4)]
        quad = [links[3, p] for p in range(4)]
        half = project(field, 3, 1)
        ahead = [[[along_x(half[s][c][r], 1) for r in range(2)] for c in range(2)] for s in range(2)]
        add_hop(total, colour_forward(quad, ahead), 3, False)
        half = colour_adjoint(quad, project(field, 3, -1))
        behind = [[[along_x(half[s][c][r], -1) for r in range(2)] for c in range(2)] for s in range(2)]
        add_hop(total, behind, 3, True)
        for s in range(4):
            for c in range(2):
                for r in range(2):
                    out[s, c, r] = total[s][c][r]
        for mu in (2, 1, 0):
            total = [[[out[s, c, r] for r in range(2)] for c in range(2)] for s in range(4)]
            for back in range(2):
                side = 2 * mu + back
                halo_copy(side, parity).wait()
                half = [[[None, None], [None, None]] for _ in range(2)]
                for s, c, r in each_part():
                    moved = hop[side, s, c, r]
                    if mu == 0:
                        halo = t_recv[parity, back, 2 * s + c] * (first_sign if back else last_sign)
                        merged = place_t(halo, moved, not back, r)
                    elif mu == 1:
                        slot = 2 * s + c
                        halo = z_recv[parity, back, r]
                        if back:
                            merged = jnp.where(z_place == 0, turned(halo, -slot, 1), moved)
                        else:
                            merged = jnp.where(z_place == nz - 1, turned(halo, nz - 1 - slot, 1), moved)
                    else:
                        slot = 4 * s + 2 * c + r
                        halo = y_recv[parity, back]
                        if back:
                            merged = jnp.where(lane < X_LEN, turned(halo, -slot * X_LEN, 2), moved)
                        else:
                            placed = turned(halo, (y_count - 1 - slot) * X_LEN, 2)
                            merged = jnp.where(lane >= width - X_LEN, placed, moved)
                    half[s][c][r] = merged
                if not back:
                    half = colour_forward([links[mu, p] for p in range(4)], half)
                add_hop(total, half, mu, back)
            for s in range(4):
                for c in range(2):
                    for r in range(2):
                        value = total[s][c][r]
                        if mu == 0:
                            value = bank[source, s, c, r] - kappa * value
                            value = value if s < 2 else -value
                        out[s, c, r] = value

    def iteration(k, carry):
        start_sum(0, sum(jnp.sum(bank[0, s] * bank[0, s], axis=(0, 1)) for s in range(4)))
        turned_wilson(0, 0)
        norm = finish_sum(0)
        growth = spread(jnp.where(k > 0, norm / ratio[...], 0.0))
        ratio[...] = norm
        square = jnp.zeros(shape, F32)
        for s in range(4):
            image = out[s] + growth * bank[1, s]
            bank[1, s] = image
            dvec[s] = bank[0, s] + growth * dvec[s]
            square = square + jnp.sum(image * image, axis=(0, 1))
        start_sum(1, square)

        @pl.when(k < ITERS - 1)
        def _():
            turned_wilson(1, 1)

        length = spread(ratio[...] / finish_sum(1))
        for s in range(4):
            xs[s] = xs[s] + length * dvec[s]
            es[s] = es[s] + length * bank[1, s]
            bank[0, s] = bank[0, s] - length * out[s]
        return carry

    lax.fori_loop(0, ITERS, iteration, 0)

    def front_copy(which):
        return pltpu.make_async_remote_copy(
            src_ref=f_send.at[which],
            dst_ref=f_recv.at[which],
            send_sem=f_ssem.at[which],
            recv_sem=f_rsem.at[which],
            device_id=step_along("ta", -1),
            device_id_type=MESH,
        )

    for which, held in enumerate((xs, es)):
        half = project({(s, c, r): held[s, c, r] for s in range(4) for c in range(2) for r in range(2)}, 0, 1)
        for s, c, moved in pack_t(half, True, f_send.at[which]):
            for r in range(2):
                hop[which, s, c, r] = moved[r]
        front_copy(which).start()
    for flavour in range(2):
        for s in range(4):
            for c in range(2):
                for r in range(2):
                    for t in range(nt):
                        sol_ref[flavour, s, c, r, t] = xs[s, c, r, flavour, t * nz : (t + 1) * nz]
    force = jnp.zeros(shape, F32)
    for which, held in enumerate((es, xs)):
        front_copy(which).wait()
        half = [[[None, None], [None, None]] for _ in range(2)]
        for s, c, r in each_part():
            half[s][c][r] = place_t(f_recv[which, 2 * s + c] * last_sign, hop[which, s, c, r], True, r)
        image = colour_forward([links[0, p] for p in range(4)], half)
        for s in range(2):
            for c in range(2):
                left = [held[s, c, r] + held[2 + s, c, r] for r in range(2)]
                term = left[1] * image[s][c][0] - left[0] * image[s][c][1]
                force = force + term if c == 0 else force - term
    force = force * (2.0 * kappa)
    force = force[0] + force[1]
    for t in range(nt):
        force_ref[t] = force[t * nz : (t + 1) * nz]


def conjugate_gradient(pseudo, gauge):
    nt, nz, width = pseudo.shape[1:]
    rows = nt * nz
    others = group_size() - 1
    field = (4, 2, 2, 2, rows, width)
    vmem = lambda *dims: pltpu.VMEM(dims, F32)
    dma = lambda *dims: pltpu.SemaphoreType.DMA(dims)
    sol, force = pl.pallas_call(
        cg_kernel,
        out_shape=(
            jax.ShapeDtypeStruct((2, 4, 2, 2, nt, nz, width), F32),
            jax.ShapeDtypeStruct((nt, nz, width), F32),
        ),
        in_specs=[pl.BlockSpec(memory_space=pltpu.VMEM)] * 2,
        out_specs=[pl.BlockSpec(memory_space=pltpu.VMEM)] * 2,
        scratch_shapes=[
            vmem(4, 4, rows, width),
            vmem(2, *field),
            vmem(*field),
            vmem(*field),
            vmem(*field),
            vmem(*field),
            vmem(6, 2, 2, 2, 2, rows, width),
            vmem(2, 4, 2, rows, width),
            vmem(2, 2, 4, 2, rows, width),
            vmem(2, 2, 2, rows, width),
            vmem(2, 2, 2, 2, rows, width),
            vmem(2, 2, rows, width),
            vmem(2, 2, 2, rows, width),
            vmem(2, 4, 2, rows, width),
            vmem(2, 4, 2, rows, width),
            vmem(8, 128),
            vmem(2, 8, 128),
            vmem(2, others, 8, 128),
            dma(6),
            dma(2, 6),
            dma(2),
            dma(2),
            dma(2, others),
            dma(2, others),
        ],
        compiler_params=pltpu.CompilerParams(
            collective_id=0, has_side_effects=True, vmem_limit_bytes=32 * 1024 * 1024
        ),
    )(pseudo.reshape((2, 4, 2, 2, nt, nz, width)), gauge.reshape((4, 4, nt, nz, width)))
    return sol.reshape(pseudo.shape), force


def sum_kernel(data_ref, out_ref, landed, reduced, ssem, rsem, gather_ssem, gather_rsem):
    count = group_size()
    chunk = data_ref.shape[0] // count
    nz, ny = lax.axis_size("gz"), lax.axis_size("gy")
    mine = (lax.axis_index("ta") * nz + lax.axis_index("gz")) * ny + lax.axis_index("gy")
    greet_group()

    def part_of(device):
        return pl.ds(pl.multiple_of(device * chunk, 8), chunk)

    def scatter(index):
        return pltpu.make_async_remote_copy(
            src_ref=data_ref.at[part_of(lax.rem(mine + index + 1, count))],
            dst_ref=landed.at[index],
            send_sem=ssem.at[index],
            recv_sem=rsem.at[index],
            device_id=peer(index + 1),
            device_id_type=MESH,
        )

    def gather(index, owner):
        return pltpu.make_async_remote_copy(
            src_ref=reduced,
            dst_ref=out_ref.at[part_of(owner)],
            send_sem=gather_ssem.at[index],
            recv_sem=gather_rsem.at[index],
            device_id=peer(index + 1),
            device_id_type=MESH,
        )

    each(count - 1, lambda index: scatter(index).start())
    each(count - 1, lambda index: scatter(index).wait())
    total = data_ref[part_of(mine)] + jnp.sum(landed[...], axis=0)
    reduced[...] = total
    each(count - 1, lambda index: gather(index, mine).start())
    out_ref[part_of(mine)] = total
    each(count - 1, lambda index: gather(index, lax.rem(mine + count - index - 1, count)).wait())


def group_sum(table):
    count = group_size()
    tiles = table.reshape((2, 8, 8, 128)).transpose((0, 2, 1, 3)).reshape((128, 128))
    chunk = -(-16 // count) * 8
    data = jnp.pad(tiles, ((0, count * chunk - 128), (0, 0)))
    dma = lambda *dims: pltpu.SemaphoreType.DMA(dims)
    summed = pl.pallas_call(
        sum_kernel,
        out_shape=jax.ShapeDtypeStruct(data.shape, F32),
        in_specs=[pl.BlockSpec(memory_space=pltpu.VMEM)],
        out_specs=pl.BlockSpec(memory_space=pltpu.VMEM),
        scratch_shapes=[
            pltpu.VMEM((count - 1, chunk, 128), F32),
            pltpu.VMEM((chunk, 128), F32),
            dma(count - 1),
            dma(count - 1),
            dma(count - 1),
            dma(count - 1),
        ],
        compiler_params=pltpu.CompilerParams(
            collective_id=1, has_side_effects=True, vmem_limit_bytes=32 * 1024 * 1024
        ),
    )(data)
    return summed[:128].reshape((2, 8, 8, 128)).transpose((0, 2, 1, 3)).reshape((16, 1024))


def tap_kernel(feature_ref, taps_ref, ext, ssem, rsem):
    nt, nz, channels, width = feature_ref.shape
    edge = 128
    for t in range(nt):
        for z in range(nz):
            ext[1 + t, 1 + z, :, edge : edge + width] = feature_ref[t, z]
    greet_group()

    def swap(index, axis, low, low_halo, high, high_halo):
        copies = []
        for side, (src, dst) in enumerate(((low, high_halo), (high, low_halo))):
            copies.append(
                pltpu.make_async_remote_copy(
                    src_ref=src,
                    dst_ref=dst,
                    send_sem=ssem.at[2 * index + side],
                    recv_sem=rsem.at[2 * index + side],
                    device_id=step_along(axis, 1 if side else -1),
                    device_id_type=MESH,
                )
            )
        for copy in copies:
            copy.start()
        for copy in copies:
            copy.wait()

    body = pl.ds(edge, width)
    mid = pl.ds(1, nz)
    swap(
        0,
        "ta",
        ext.at[1, mid, :, body],
        ext.at[0, mid, :, body],
        ext.at[nt, mid, :, body],
        ext.at[nt + 1, mid, :, body],
    )
    swap(
        1,
        "gz",
        ext.at[:, 1, :, body],
        ext.at[:, 0, :, body],
        ext.at[:, nz, :, body],
        ext.at[:, nz + 1, :, body],
    )
    swap(
        2,
        "gy",
        ext.at[:, :, :, pl.ds(edge, edge)],
        ext.at[:, :, :, pl.ds(0, edge)],
        ext.at[:, :, :, pl.ds(width, edge)],
        ext.at[:, :, :, pl.ds(edge + width, edge)],
    )
    for tt in range(nt + 2):
        for zz in range(nz + 2):
            cells = ext[tt, zz]
            for oy in (-1, 0, 1):
                base = turned(cells, -(edge + X_LEN * oy), 1)[:, 0:width]
                for ox in (-1, 0, 1):
                    tile = base if ox == 0 else along_x(base, ox)
                    for ot in (-1, 0, 1):
                        for oz in (-1, 0, 1):
                            t, z = tt - 1 - ot, zz - 1 - oz
                            if 0 <= t < nt and 0 <= z < nz:
                                tap = 27 * (ot + 1) + 9 * (oz + 1) + 3 * (oy + 1) + ox + 1
                                start = (t * nz + z) * width
                                taps_ref[tap * channels : (tap + 1) * channels, start : start + width] = tile


def conditioner_taps(features):
    nt, nz, channels, width = features.shape
    return pl.pallas_call(
        tap_kernel,
        out_shape=jax.ShapeDtypeStruct((81 * channels, nt * nz * width), F32),
        in_specs=[pl.BlockSpec(memory_space=pltpu.VMEM)],
        out_specs=pl.BlockSpec(memory_space=pltpu.VMEM),
        scratch_shapes=[
            pltpu.VMEM((nt + 2, nz + 2, channels, width + 256), F32),
            pltpu.SemaphoreType.DMA((6,)),
            pltpu.SemaphoreType.DMA((6,)),
        ],
        compiler_params=pltpu.CompilerParams(
            collective_id=2, has_side_effects=True, vmem_limit_bytes=32 * 1024 * 1024
        ),
    )(features)


def on_device(pseudo, frame_quat, link_phase, active, kernel, bias_hidden, readout, bias_out):
    scale = SLOPE_SHARE * 2.0 * math.pi / KNOTS
    ratio = KNOTS / (2.0 * math.pi)
    mask = active.astype(F32).reshape((-1,))
    taps = conditioner_taps(conditioner_inputs(link_phase, active).transpose((1, 2, 0, 3)))
    summed = jnp.einsum("ti,ts->is", kernel, taps, precision=lax.Precision.HIGH)
    hidden = jnp.tanh(summed + bias_hidden[:, None])
    logits = jnp.einsum("ik,is->ks", readout, hidden, precision=PRECISE)
    squashed = jnp.tanh(logits + bias_out[:, None])
    coeffs = scale * squashed
    angle = link_phase[0].reshape((-1,))
    values, slopes = spline_basis(angle)
    moved = angle + mask * jnp.sum(coeffs * values, axis=0)
    jacobian = 1.0 + mask * ratio * jnp.sum(coeffs * slopes, axis=0)
    angles = jnp.concatenate([moved.reshape((1,) + active.shape), link_phase[1:]], axis=0)
    solution, force_field = conjugate_gradient(pseudo, rotate_links(frame_quat, angles))
    root_volume = math.sqrt(active.size * group_size())
    force = force_field.reshape((-1,))
    coeff_grad = mask * (force * values - ratio * slopes / jacobian) / root_volume
    logit_grad = coeff_grad * scale * (1.0 - squashed * squashed)
    pre_grad = jnp.einsum("ik,ks->is", readout, logit_grad, precision=PRECISE) * (1.0 - hidden * hidden)
    kernel_part = jnp.einsum("is,ts->it", pre_grad, taps, precision=lax.Precision.HIGH)
    readout_part = jnp.einsum("is,ks->ik", hidden, logit_grad, precision=PRECISE)
    hidden_part = jnp.sum(pre_grad, axis=1, keepdims=True)
    out_part = jnp.pad(jnp.sum(logit_grad, axis=1, keepdims=True), ((0, 16 - KNOTS), (0, 0)))
    n = kernel.shape[0]
    table = jnp.concatenate([kernel_part, readout_part, hidden_part, out_part], axis=1)
    table = group_sum(jnp.pad(table, ((0, 0), (0, 1024 - table.shape[1]))))
    return (
        solution,
        force_field,
        table[:, :n].T,
        table[:, n + KNOTS],
        table[:, n : n + KNOTS],
        table[:KNOTS, n + KNOTS + 1],
    )


def solution(mesh):
    return jax.shard_map(
        on_device,
        mesh=mesh,
        in_specs=(
            P("groups", "ta", "gz", "gy"),
            P("groups", "ta", "gz", "gy"),
            P("groups", "ta", "gz", "gy"),
            P(("groups", "ta"), "gz", "gy"),
            P(),
            P(),
            P(),
            P(),
        ),
        out_specs=(
            P("groups", "ta", "gz", "gy"),
            P(("groups", "ta"), "gz", "gy"),
            P("groups", None),
            P("groups"),
            P("groups", None),
            P("groups"),
        ),
        check_vma=False,
    )
```

```python
import math

import jax
import jax.numpy as jnp
from jax import lax
from jax.experimental import pallas as pl
from jax.experimental.pallas import tpu as pltpu
from jax.sharding import PartitionSpec as P

X_LEN = 32
ITERS = 3
KNOTS = 8


PRECISE = lax.Precision.HIGHEST
KAPPAS = (0.12, 0.1)
SLOPE_SHARE = 0.5


def rotate_one(quadruple, theta_field):
    cosine = jnp.cos(theta_field)
    sine_part = jnp.sin(theta_field)
    return jnp.stack(
        [
            cosine * quadruple[0] - sine_part * quadruple[1],
            cosine * quadruple[1] + sine_part * quadruple[0],
            cosine * quadruple[2] - sine_part * quadruple[3],
            cosine * quadruple[3] + sine_part * quadruple[2],
        ],
        axis=0,
    )


def rotate_links(frame_quat, angles):
    return jnp.concatenate(
        [
            rotate_one(frame_quat[4 * direction : 4 * direction + 4], angles[direction])
            for direction in range(4)
        ],
        axis=0,
    )


def bspline(offsets):
    distance = jnp.abs(offsets)
    outer_part = jnp.maximum(2.0 - distance, 0.0)
    inner_part = jnp.maximum(1.0 - distance, 0.0)
    return (outer_part**3 - 4.0 * inner_part**3) / 6.0


def bspline_slope(offsets):
    distance = jnp.abs(offsets)
    outer_part = jnp.maximum(2.0 - distance, 0.0)
    inner_part = jnp.maximum(1.0 - distance, 0.0)
    return jnp.sign(offsets) * (4.0 * inner_part**2 - outer_part**2) / 2.0


def spline_basis(time_angle):
    position = KNOTS * (time_angle + math.pi) / (2.0 * math.pi)
    knot_index = jnp.arange(KNOTS, dtype=jnp.float32).reshape((KNOTS,) + (1,) * time_angle.ndim)
    offsets = jnp.mod(position[None] - knot_index + KNOTS / 2.0, KNOTS) - KNOTS / 2.0
    return (bspline(offsets), bspline_slope(offsets))


def conditioner_inputs(link_phase, active):
    frozen = 1.0 - active.astype(jnp.float32)
    channels = []
    for direction in range(4):
        if direction == 0:
            channels.append(jnp.cos(link_phase[direction]) * frozen)
            channels.append(jnp.sin(link_phase[direction]) * frozen)
        else:
            channels.append(jnp.cos(link_phase[direction]))
            channels.append(jnp.sin(link_phase[direction]))
    return jnp.stack(channels, axis=0)


GROUP = ("ta", "gz", "gy")
MESH = pl.DeviceIdType.MESH
F32 = jnp.float32

SPIN_K = {
    1: [[(-1, 0, 1), (1, 0, 0)], [(1, 1, 1), (-1, 1, 0)]],
    2: [[(1, 1, 0), (1, 1, 1)], [(-1, 0, 0), (-1, 0, 1)]],
    3: [[(-1, 1, 1), (1, 1, 0)], [(-1, 0, 1), (1, 0, 0)]],
}
TURN = {0: [[(-1, 0, 0), (-1, 0, 1)], [(-1, 1, 0), (-1, 1, 1)]], **SPIN_K}
BACK = {0: [[(1, 0, 0), (1, 0, 1)], [(1, 1, 0), (1, 1, 1)]], **SPIN_K}


def group_size():
    return lax.axis_size("ta") * lax.axis_size("gz") * lax.axis_size("gy")


def each(count, step):
    if count <= 16:
        for index in range(count):
            step(index)
    else:

        def looped(index, carry):
            step(index)
            return carry

        lax.fori_loop(0, count, looped, 0)


def plane_size():
    return lax.axis_size("gz") * lax.axis_size("gy")


def plane_place():
    return lax.axis_index("gz") * lax.axis_size("gy") + lax.axis_index("gy")


def plane_peer(offset):
    ny = lax.axis_size("gy")
    target = lax.rem(plane_place() + offset, plane_size())
    return {"gz": target // ny, "gy": lax.rem(target, ny)}


def time_peer(offset):
    return {"ta": lax.rem(lax.axis_index("ta") + offset, lax.axis_size("ta"))}


def greet_lines():
    barrier = pltpu.get_barrier_semaphore()
    planes, times = plane_size() - 1, lax.axis_size("ta") - 1
    for count, partner in ((planes, plane_peer), (times, time_peer)):

        def greet(index):
            pl.semaphore_signal(barrier, inc=1, device_id=partner(index + 1), device_id_type=MESH)

        each(count, greet)
    pl.semaphore_wait(barrier, planes + times)


def step_along(axis, distance):
    count = lax.axis_size(axis)
    return {axis: lax.rem(lax.axis_index(axis) + (distance + count), count)}


def rows_of(shape):
    return lax.broadcasted_iota(jnp.int32, shape, len(shape) - 2)


def lanes_of(shape):
    return lax.broadcasted_iota(jnp.int32, shape, len(shape) - 1)


def turned(tensor, shift, axis):
    size = tensor.shape[axis]
    shift = shift % size
    return tensor if shift == 0 else pltpu.roll(tensor, shift, axis)


def colour_forward(quad, half):
    a_re, a_im, b_re, b_im = quad
    result = []
    for spin in range(2):
        (u_re, u_im), (l_re, l_im) = half[spin]
        result.append(
            [
                [
                    a_re * u_re - a_im * u_im + b_re * l_re - b_im * l_im,
                    a_re * u_im + a_im * u_re + b_re * l_im + b_im * l_re,
                ],
                [
                    a_re * l_re + a_im * l_im - b_re * u_re - b_im * u_im,
                    a_re * l_im - a_im * l_re - b_re * u_im + b_im * u_re,
                ],
            ]
        )
    return result


def colour_adjoint(quad, half):
    a_re, a_im, b_re, b_im = quad
    result = []
    for spin in range(2):
        (u_re, u_im), (l_re, l_im) = half[spin]
        result.append(
            [
                [
                    a_re * u_re + a_im * u_im - b_re * l_re + b_im * l_im,
                    a_re * u_im - a_im * u_re - b_re * l_im - b_im * l_re,
                ],
                [
                    b_re * u_re + b_im * u_im + a_re * l_re - a_im * l_im,
                    b_re * u_im - b_im * u_re + a_re * l_im + a_im * l_re,
                ],
            ]
        )
    return result


def project(field, mu, sign):
    half = []
    for spin in range(2):
        colours = []
        for colour in range(2):
            parts = []
            for part in range(2):
                flip, s, r = TURN[mu][spin][part]
                upper, lower = field[spin, colour, part], field[2 + s, colour, r]
                parts.append(upper + lower if flip * sign > 0 else upper - lower)
            colours.append(parts)
        half.append(colours)
    return half


def along_x(tensor, stride):
    axis = tensor.ndim - 1
    place = lax.rem(lanes_of(tensor.shape), X_LEN)
    wrap = X_LEN - 1
    if stride > 0:
        return jnp.where(place == wrap, turned(tensor, wrap, axis), turned(tensor, -1, axis))
    return jnp.where(place == 0, turned(tensor, -wrap, axis), turned(tensor, 1, axis))


def each_part():
    return [(s, c, r) for s in range(2) for c in range(2) for r in range(2)]


def cg_kernel(
    pseudo_ref,
    gauge_ref,
    sol_ref,
    force_ref,
    links,
    bank,
    dvec,
    xs,
    es,
    out,
    hop,
    t_send,
    t_recv,
    z_send,
    z_recv,
    y_send,
    y_recv,
    f_send,
    f_recv,
    ratio,
    red_send,
    red_recv,
    line_send,
    line_recv,
    halo_ssem,
    halo_rsem,
    f_ssem,
    f_rsem,
    red_ssem,
    red_rsem,
    line_ssem,
    line_rsem,
):
    nt, nz, width = pseudo_ref.shape[-3:]
    shape = (2, nt * nz, width)
    planes, times = plane_size() - 1, lax.axis_size("ta") - 1
    row, lane = rows_of(shape), lanes_of(shape)
    z_place = lax.rem(row, nz)
    t_low = row < (nt - 1) * nz
    y_count = width // X_LEN
    kappa = jnp.where(lax.broadcasted_iota(jnp.int32, shape, 0) == 0, KAPPAS[0], KAPPAS[1]).astype(F32)
    last_sign = jnp.where(lax.axis_index("ta") == lax.axis_size("ta") - 1, -1.0, 1.0).astype(F32)
    first_sign = jnp.where(lax.axis_index("ta") == 0, -1.0, 1.0).astype(F32)

    for mu in range(4):
        for part in range(4):
            for t in range(nt):
                links[mu, part, t * nz : (t + 1) * nz] = gauge_ref[mu, part, t]
    for flavour in range(2):
        for s in range(4):
            for c in range(2):
                for r in range(2):
                    for t in range(nt):
                        rows = slice(t * nz, (t + 1) * nz)
                        bank[0, s, c, r, flavour, rows] = pseudo_ref[flavour, s, c, r, t]
    for s in range(4):
        zero = jnp.zeros((2, 2) + shape, F32)
        bank[1, s] = zero
        dvec[s] = zero
        xs[s] = zero
        es[s] = zero
        out[s] = zero
    ratio[...] = jnp.ones(ratio.shape, F32)

    greet_lines()

    def reduce_copy(parity, index):
        return pltpu.make_async_remote_copy(
            src_ref=red_send.at[parity],
            dst_ref=red_recv.at[parity, index],
            send_sem=red_ssem.at[parity, index],
            recv_sem=red_rsem.at[parity, index],
            device_id=plane_peer(index + 1),
            device_id_type=MESH,
        )

    def line_copy(parity, index):
        return pltpu.make_async_remote_copy(
            src_ref=line_send.at[parity],
            dst_ref=line_recv.at[parity, index],
            send_sem=line_ssem.at[parity, index],
            recv_sem=line_rsem.at[parity, index],
            device_id=time_peer(index + 1),
            device_id_type=MESH,
        )

    def start_sum(parity, total):
        folded = total[:, :, 0:128]
        for start in range(128, width, 128):
            folded = folded + total[:, :, start : start + 128]
        sums = jnp.sum(folded, axis=1, keepdims=True)
        tile_row = rows_of((8, 128))
        red_send[parity] = jnp.where(tile_row == 0, sums[0], jnp.where(tile_row == 1, sums[1], 0.0))
        each(planes, lambda index: reduce_copy(parity, index).start())

    def pass_sum(parity):
        each(planes, lambda index: reduce_copy(parity, index).wait())
        line_send[parity] = red_send[parity] + jnp.sum(red_recv[parity], axis=0)
        each(times, lambda index: line_copy(parity, index).start())

    def finish_sum(parity):
        each(times, lambda index: line_copy(parity, index).wait())
        total = line_send[parity] + jnp.sum(line_recv[parity], axis=0)
        total = jnp.broadcast_to(jnp.sum(total, axis=1, keepdims=True), (8, 128))
        return jnp.where(rows_of((8, 128)) < 2, total, 1.0)

    def spread(pair):
        return jnp.stack([jnp.broadcast_to(pair[f : f + 1, 0:1], shape[1:]) for f in range(2)])

    def halo_copy(side, parity):
        send, recv, axis = ((t_send, t_recv, "ta"), (z_send, z_recv, "gz"), (y_send, y_recv, "gy"))[side // 2]
        return pltpu.make_async_remote_copy(
            src_ref=send.at[side % 2],
            dst_ref=recv.at[parity, side % 2],
            send_sem=halo_ssem.at[side],
            recv_sem=halo_rsem.at[parity, side],
            device_id=step_along(axis, -1 if side % 2 == 0 else 1),
            device_id_type=MESH,
        )

    def pack_t(half, ahead, send):
        for s, c in ((0, 0), (0, 1), (1, 0), (1, 1)):
            first, second = half[s][c]
            moved = [turned(v, -nz if ahead else nz, 1) for v in (first, second)]
            if ahead:
                send[2 * s + c] = jnp.where(row < nz, second, moved[0]) if nt == 2 else None
            else:
                send[2 * s + c] = jnp.where(row < nz, moved[0], second)
            yield s, c, moved

    def place_t(halo, moved, ahead, part):
        if ahead:
            edge = halo if part == 0 else turned(halo, nz, 1)
            return jnp.where(t_low, moved, edge)
        edge = halo if part == 0 else turned(halo, nz, 1)
        return jnp.where(row < nz, edge, moved)

    def send_halos(field, parity):
        for mu in range(3):
            for back in range(2):
                half = project(field, mu, -1 if back else 1)
                if back:
                    half = colour_adjoint([links[mu, p] for p in range(4)], half)
                side = 2 * mu + back
                if mu == 0:
                    for s, c, moved in pack_t(half, not back, t_send.at[back]):
                        for r in range(2):
                            hop[side, s, c, r] = moved[r]
                elif mu == 1:
                    packed = [None, None]
                    for s, c, r in each_part():
                        value = half[s][c][r]
                        hop[side, s, c, r] = turned(value, 1 if back else -1, 1)
                        slot = 2 * s + c
                        put = turned(value, slot - (nz - 1) if back else slot, 1)
                        packed[r] = put if packed[r] is None else jnp.where(z_place == slot, put, packed[r])
                    for r in range(2):
                        z_send[back, r] = packed[r]
                else:
                    packed = None
                    for s, c, r in each_part():
                        value = half[s][c][r]
                        hop[side, s, c, r] = turned(value, X_LEN if back else -X_LEN, 2)
                        slot = 4 * s + 2 * c + r
                        put = turned(value, (slot - (y_count - 1) if back else slot) * X_LEN, 2)
                        packed = put if packed is None else jnp.where(lane // X_LEN == slot, put, packed)
                    y_send[back] = packed
                halo_copy(side, parity).start()

    def add_hop(total, half, mu, back):
        sign = 1 if back else -1
        for s, c, r in each_part():
            flip, source, part = BACK[mu][s][r]
            top, low = half[s][c][r], half[source][c][part]
            if total[s][c][r] is None:
                total[s][c][r] = top
                total[2 + s][c][r] = low if flip * sign > 0 else -low
            else:
                total[s][c][r] = total[s][c][r] + top
                lower = total[2 + s][c][r]
                total[2 + s][c][r] = lower + low if flip * sign > 0 else lower - low

    def turned_wilson(source, parity):
        field = {
            (s, c, r): bank[source, s, c, r] for s in range(4) for c in range(2) for r in range(2)
        }
        send_halos(field, parity)
        total = [[[None, None], [None, None]] for _ in range(4)]
        quad = [links[3, p] for p in range(4)]
        half = project(field, 3, 1)
        ahead = [[[along_x(half[s][c][r], 1) for r in range(2)] for c in range(2)] for s in range(2)]
        add_hop(total, colour_forward(quad, ahead), 3, False)
        half = colour_adjoint(quad, project(field, 3, -1))
        behind = [[[along_x(half[s][c][r], -1) for r in range(2)] for c in range(2)] for s in range(2)]
        add_hop(total, behind, 3, True)
        for s in range(4):
            for c in range(2):
                for r in range(2):
                    out[s, c, r] = total[s][c][r]
        pass_sum(parity)
        for mu in (2, 1, 0):
            total = [[[out[s, c, r] for r in range(2)] for c in range(2)] for s in range(4)]
            for back in range(2):
                side = 2 * mu + back
                halo_copy(side, parity).wait()
                half = [[[None, None], [None, None]] for _ in range(2)]
                for s, c, r in each_part():
                    moved = hop[side, s, c, r]
                    if mu == 0:
                        halo = t_recv[parity, back, 2 * s + c] * (first_sign if back else last_sign)
                        merged = place_t(halo, moved, not back, r)
                    elif mu == 1:
                        slot = 2 * s + c
                        halo = z_recv[parity, back, r]
                        if back:
                            merged = jnp.where(z_place == 0, turned(halo, -slot, 1), moved)
                        else:
                            merged = jnp.where(z_place == nz - 1, turned(halo, nz - 1 - slot, 1), moved)
                    else:
                        slot = 4 * s + 2 * c + r
                        halo = y_recv[parity, back]
                        if back:
                            merged = jnp.where(lane < X_LEN, turned(halo, -slot * X_LEN, 2), moved)
                        else:
                            placed = turned(halo, (y_count - 1 - slot) * X_LEN, 2)
                            merged = jnp.where(lane >= width - X_LEN, placed, moved)
                    half[s][c][r] = merged
                if not back:
                    half = colour_forward([links[mu, p] for p in range(4)], half)
                add_hop(total, half, mu, back)
            for s in range(4):
                for c in range(2):
                    for r in range(2):
                        value = total[s][c][r]
                        if mu == 0:
                            value = bank[source, s, c, r] - kappa * value
                            value = value if s < 2 else -value
                        out[s, c, r] = value

    def iteration(k, carry):
        start_sum(0, sum(jnp.sum(bank[0, s] * bank[0, s], axis=(0, 1)) for s in range(4)))
        turned_wilson(0, 0)
        norm = finish_sum(0)
        growth = spread(jnp.where(k > 0, norm / ratio[...], 0.0))
        ratio[...] = norm
        square = jnp.zeros(shape, F32)
        for s in range(4):
            image = out[s] + growth * bank[1, s]
            bank[1, s] = image
            dvec[s] = bank[0, s] + growth * dvec[s]
            square = square + jnp.sum(image * image, axis=(0, 1))
        start_sum(1, square)

        @pl.when(k < ITERS - 1)
        def _():
            turned_wilson(1, 1)

        @pl.when(k == ITERS - 1)
        def _():
            pass_sum(1)

        length = spread(ratio[...] / finish_sum(1))
        for s in range(4):
            xs[s] = xs[s] + length * dvec[s]
            es[s] = es[s] + length * bank[1, s]
            bank[0, s] = bank[0, s] - length * out[s]
        return carry

    lax.fori_loop(0, ITERS, iteration, 0)

    def front_copy(which):
        return pltpu.make_async_remote_copy(
            src_ref=f_send.at[which],
            dst_ref=f_recv.at[which],
            send_sem=f_ssem.at[which],
            recv_sem=f_rsem.at[which],
            device_id=step_along("ta", -1),
            device_id_type=MESH,
        )

    for which, held in enumerate((xs, es)):
        half = project({(s, c, r): held[s, c, r] for s in range(4) for c in range(2) for r in range(2)}, 0, 1)
        for s, c, moved in pack_t(half, True, f_send.at[which]):
            for r in range(2):
                hop[which, s, c, r] = moved[r]
        front_copy(which).start()
    for flavour in range(2):
        for s in range(4):
            for c in range(2):
                for r in range(2):
                    for t in range(nt):
                        sol_ref[flavour, s, c, r, t] = xs[s, c, r, flavour, t * nz : (t + 1) * nz]
    force = jnp.zeros(shape, F32)
    for which, held in enumerate((es, xs)):
        front_copy(which).wait()
        half = [[[None, None], [None, None]] for _ in range(2)]
        for s, c, r in each_part():
            half[s][c][r] = place_t(f_recv[which, 2 * s + c] * last_sign, hop[which, s, c, r], True, r)
        image = colour_forward([links[0, p] for p in range(4)], half)
        for s in range(2):
            for c in range(2):
                left = [held[s, c, r] + held[2 + s, c, r] for r in range(2)]
                term = left[1] * image[s][c][0] - left[0] * image[s][c][1]
                force = force + term if c == 0 else force - term
    force = force * (2.0 * kappa)
    force = force[0] + force[1]
    for t in range(nt):
        force_ref[t] = force[t * nz : (t + 1) * nz]


def conjugate_gradient(pseudo, gauge):
    nt, nz, width = pseudo.shape[1:]
    rows = nt * nz
    planes, times = plane_size() - 1, lax.axis_size("ta") - 1
    field = (4, 2, 2, 2, rows, width)
    vmem = lambda *dims: pltpu.VMEM(dims, F32)
    dma = lambda *dims: pltpu.SemaphoreType.DMA(dims)
    sol, force = pl.pallas_call(
        cg_kernel,
        out_shape=(
            jax.ShapeDtypeStruct((2, 4, 2, 2, nt, nz, width), F32),
            jax.ShapeDtypeStruct((nt, nz, width), F32),
        ),
        in_specs=[pl.BlockSpec(memory_space=pltpu.VMEM)] * 2,
        out_specs=[pl.BlockSpec(memory_space=pltpu.VMEM)] * 2,
        scratch_shapes=[
            vmem(4, 4, rows, width),
            vmem(2, *field),
            vmem(*field),
            vmem(*field),
            vmem(*field),
            vmem(*field),
            vmem(6, 2, 2, 2, 2, rows, width),
            vmem(2, 4, 2, rows, width),
            vmem(2, 2, 4, 2, rows, width),
            vmem(2, 2, 2, rows, width),
            vmem(2, 2, 2, 2, rows, width),
            vmem(2, 2, rows, width),
            vmem(2, 2, 2, rows, width),
            vmem(2, 4, 2, rows, width),
            vmem(2, 4, 2, rows, width),
            vmem(8, 128),
            vmem(2, 8, 128),
            vmem(2, planes, 8, 128),
            vmem(2, 8, 128),
            vmem(2, times, 8, 128),
            dma(6),
            dma(2, 6),
            dma(2),
            dma(2),
            dma(2, planes),
            dma(2, planes),
            dma(2, times),
            dma(2, times),
        ],
        compiler_params=pltpu.CompilerParams(
            collective_id=0, has_side_effects=True, vmem_limit_bytes=32 * 1024 * 1024
        ),
    )(pseudo.reshape((2, 4, 2, 2, nt, nz, width)), gauge.reshape((4, 4, nt, nz, width)))
    return sol.reshape(pseudo.shape), force


def sum_kernel(data_ref, out_ref, landed, lined, reduced, *sems):
    planes, times = plane_size(), lax.axis_size("ta")
    chunk = data_ref.shape[0] // planes
    place, now = plane_place(), lax.axis_index("ta")
    greet_lines()

    def part_of(device):
        return pl.ds(pl.multiple_of(device * chunk, 8), chunk)

    def copy(stage, index, src, dst, target):
        return pltpu.make_async_remote_copy(
            src_ref=src,
            dst_ref=dst,
            send_sem=sems[2 * stage].at[index],
            recv_sem=sems[2 * stage + 1].at[index],
            device_id=target,
            device_id_type=MESH,
        )

    def scatter(index):
        src = data_ref.at[part_of(lax.rem(place + index + 1, planes))]
        return copy(0, index, src, landed.at[index], plane_peer(index + 1))

    def across(index, owner):
        return copy(1, index, reduced.at[0], lined.at[owner], time_peer(index + 1))

    def gather(index, owner):
        return copy(2, index, reduced.at[1], out_ref.at[part_of(owner)], plane_peer(index + 1))

    each(planes - 1, lambda index: scatter(index).start())
    each(planes - 1, lambda index: scatter(index).wait())
    partial = data_ref[part_of(place)] + jnp.sum(landed[...], axis=0)
    reduced[0] = partial
    each(times - 1, lambda index: across(index, now).start())
    lined[now] = partial
    each(times - 1, lambda index: across(index, lax.rem(now + times - index - 1, times)).wait())
    total = jnp.sum(lined[...], axis=0)
    reduced[1] = total
    each(planes - 1, lambda index: gather(index, place).start())
    out_ref[part_of(place)] = total
    each(planes - 1, lambda index: gather(index, lax.rem(place + planes - index - 1, planes)).wait())


def group_sum(table):
    planes, times = plane_size(), lax.axis_size("ta")
    tiles = table.reshape((2, 8, 8, 128)).transpose((0, 2, 1, 3)).reshape((128, 128))
    chunk = -(-16 // planes) * 8
    data = jnp.pad(tiles, ((0, planes * chunk - 128), (0, 0)))
    counts = (planes - 1, planes - 1, times - 1, times - 1, planes - 1, planes - 1)
    summed = pl.pallas_call(
        sum_kernel,
        out_shape=jax.ShapeDtypeStruct(data.shape, F32),
        in_specs=[pl.BlockSpec(memory_space=pltpu.VMEM)],
        out_specs=pl.BlockSpec(memory_space=pltpu.VMEM),
        scratch_shapes=[
            pltpu.VMEM((planes - 1, chunk, 128), F32),
            pltpu.VMEM((times, chunk, 128), F32),
            pltpu.VMEM((2, chunk, 128), F32),
            *[pltpu.SemaphoreType.DMA((count,)) for count in counts],
        ],
        compiler_params=pltpu.CompilerParams(
            collective_id=1, has_side_effects=True, vmem_limit_bytes=32 * 1024 * 1024
        ),
    )(data)
    return summed[:128].reshape((2, 8, 8, 128)).transpose((0, 2, 1, 3)).reshape((16, 1024))


def tap_kernel(feature_ref, taps_ref, ext, ssem, rsem):
    nt, nz, channels, width = feature_ref.shape
    edge = 128
    for t in range(nt):
        for z in range(nz):
            ext[1 + t, 1 + z, :, edge : edge + width] = feature_ref[t, z]
    greet_lines()

    def swap(index, axis, low, low_halo, high, high_halo):
        copies = []
        for side, (src, dst) in enumerate(((low, high_halo), (high, low_halo))):
            copies.append(
                pltpu.make_async_remote_copy(
                    src_ref=src,
                    dst_ref=dst,
                    send_sem=ssem.at[2 * index + side],
                    recv_sem=rsem.at[2 * index + side],
                    device_id=step_along(axis, 1 if side else -1),
                    device_id_type=MESH,
                )
            )
        for copy in copies:
            copy.start()
        for copy in copies:
            copy.wait()

    body = pl.ds(edge, width)
    mid = pl.ds(1, nz)
    swap(
        0,
        "ta",
        ext.at[1, mid, :, body],
        ext.at[0, mid, :, body],
        ext.at[nt, mid, :, body],
        ext.at[nt + 1, mid, :, body],
    )
    swap(
        1,
        "gz",
        ext.at[:, 1, :, body],
        ext.at[:, 0, :, body],
        ext.at[:, nz, :, body],
        ext.at[:, nz + 1, :, body],
    )
    swap(
        2,
        "gy",
        ext.at[:, :, :, pl.ds(edge, edge)],
        ext.at[:, :, :, pl.ds(0, edge)],
        ext.at[:, :, :, pl.ds(width, edge)],
        ext.at[:, :, :, pl.ds(edge + width, edge)],
    )
    for tt in range(nt + 2):
        for zz in range(nz + 2):
            cells = ext[tt, zz]
            for oy in (-1, 0, 1):
                base = turned(cells, -(edge + X_LEN * oy), 1)[:, 0:width]
                for ox in (-1, 0, 1):
                    tile = base if ox == 0 else along_x(base, ox)
                    for ot in (-1, 0, 1):
                        for oz in (-1, 0, 1):
                            t, z = tt - 1 - ot, zz - 1 - oz
                            if 0 <= t < nt and 0 <= z < nz:
                                tap = 27 * (ot + 1) + 9 * (oz + 1) + 3 * (oy + 1) + ox + 1
                                start = (t * nz + z) * width
                                taps_ref[tap * channels : (tap + 1) * channels, start : start + width] = tile


def conditioner_taps(features):
    nt, nz, channels, width = features.shape
    return pl.pallas_call(
        tap_kernel,
        out_shape=jax.ShapeDtypeStruct((81 * channels, nt * nz * width), F32),
        in_specs=[pl.BlockSpec(memory_space=pltpu.VMEM)],
        out_specs=pl.BlockSpec(memory_space=pltpu.VMEM),
        scratch_shapes=[
            pltpu.VMEM((nt + 2, nz + 2, channels, width + 256), F32),
            pltpu.SemaphoreType.DMA((6,)),
            pltpu.SemaphoreType.DMA((6,)),
        ],
        compiler_params=pltpu.CompilerParams(
            collective_id=2, has_side_effects=True, vmem_limit_bytes=32 * 1024 * 1024
        ),
    )(features)


def on_device(pseudo, frame_quat, link_phase, active, kernel, bias_hidden, readout, bias_out):
    scale = SLOPE_SHARE * 2.0 * math.pi / KNOTS
    ratio = KNOTS / (2.0 * math.pi)
    mask = active.astype(F32).reshape((-1,))
    taps = conditioner_taps(conditioner_inputs(link_phase, active).transpose((1, 2, 0, 3)))
    summed = jnp.einsum("ti,ts->is", kernel, taps, precision=lax.Precision.HIGH)
    hidden = jnp.tanh(summed + bias_hidden[:, None])
    logits = jnp.einsum("ik,is->ks", readout, hidden, precision=PRECISE)
    squashed = jnp.tanh(logits + bias_out[:, None])
    coeffs = scale * squashed
    angle = link_phase[0].reshape((-1,))
    values, slopes = spline_basis(angle)
    moved = angle + mask * jnp.sum(coeffs * values, axis=0)
    jacobian = 1.0 + mask * ratio * jnp.sum(coeffs * slopes, axis=0)
    angles = jnp.concatenate([moved.reshape((1,) + active.shape), link_phase[1:]], axis=0)
    solution, force_field = conjugate_gradient(pseudo, rotate_links(frame_quat, angles))
    root_volume = math.sqrt(active.size * group_size())
    force = force_field.reshape((-1,))
    coeff_grad = mask * (force * values - ratio * slopes / jacobian) / root_volume
    logit_grad = coeff_grad * scale * (1.0 - squashed * squashed)
    pre_grad = jnp.einsum("ik,ks->is", readout, logit_grad, precision=PRECISE) * (1.0 - hidden * hidden)
    kernel_part = jnp.einsum("is,ts->it", pre_grad, taps, precision=lax.Precision.HIGH)
    readout_part = jnp.einsum("is,ks->ik", hidden, logit_grad, precision=PRECISE)
    hidden_part = jnp.sum(pre_grad, axis=1, keepdims=True)
    out_part = jnp.pad(jnp.sum(logit_grad, axis=1, keepdims=True), ((0, 16 - KNOTS), (0, 0)))
    n = kernel.shape[0]
    table = jnp.concatenate([kernel_part, readout_part, hidden_part, out_part], axis=1)
    table = group_sum(jnp.pad(table, ((0, 0), (0, 1024 - table.shape[1]))))
    return (
        solution,
        force_field,
        table[:, :n].T,
        table[:, n + KNOTS],
        table[:, n : n + KNOTS],
        table[:KNOTS, n + KNOTS + 1],
    )


def solution(mesh):
    return jax.shard_map(
        on_device,
        mesh=mesh,
        in_specs=(
            P("groups", "ta", "gz", "gy"),
            P("groups", "ta", "gz", "gy"),
            P("groups", "ta", "gz", "gy"),
            P(("groups", "ta"), "gz", "gy"),
            P(),
            P(),
            P(),
            P(),
        ),
        out_specs=(
            P("groups", "ta", "gz", "gy"),
            P(("groups", "ta"), "gz", "gy"),
            P("groups", None),
            P("groups"),
            P("groups", None),
            P("groups"),
        ),
        check_vma=False,
    )
```

```python
import math

import jax
import jax.numpy as jnp
from jax import lax
from jax.experimental import pallas as pl
from jax.experimental.pallas import tpu as pltpu
from jax.sharding import PartitionSpec as P

X_LEN = 32
ITERS = 3
KNOTS = 8


PRECISE = lax.Precision.HIGHEST
KAPPAS = (0.12, 0.1)
SLOPE_SHARE = 0.5


def rotate_one(quadruple, theta_field):
    cosine = jnp.cos(theta_field)
    sine_part = jnp.sin(theta_field)
    return jnp.stack(
        [
            cosine * quadruple[0] - sine_part * quadruple[1],
            cosine * quadruple[1] + sine_part * quadruple[0],
            cosine * quadruple[2] - sine_part * quadruple[3],
            cosine * quadruple[3] + sine_part * quadruple[2],
        ],
        axis=0,
    )


def rotate_links(frame_quat, angles):
    return jnp.concatenate(
        [
            rotate_one(frame_quat[4 * direction : 4 * direction + 4], angles[direction])
            for direction in range(4)
        ],
        axis=0,
    )


def bspline(offsets):
    distance = jnp.abs(offsets)
    outer_part = jnp.maximum(2.0 - distance, 0.0)
    inner_part = jnp.maximum(1.0 - distance, 0.0)
    return (outer_part**3 - 4.0 * inner_part**3) / 6.0


def bspline_slope(offsets):
    distance = jnp.abs(offsets)
    outer_part = jnp.maximum(2.0 - distance, 0.0)
    inner_part = jnp.maximum(1.0 - distance, 0.0)
    return jnp.sign(offsets) * (4.0 * inner_part**2 - outer_part**2) / 2.0


def spline_basis(time_angle):
    position = KNOTS * (time_angle + math.pi) / (2.0 * math.pi)
    knot_index = jnp.arange(KNOTS, dtype=jnp.float32).reshape((KNOTS,) + (1,) * time_angle.ndim)
    offsets = jnp.mod(position[None] - knot_index + KNOTS / 2.0, KNOTS) - KNOTS / 2.0
    return (bspline(offsets), bspline_slope(offsets))


def conditioner_inputs(link_phase, active):
    frozen = 1.0 - active.astype(jnp.float32)
    channels = []
    for direction in range(4):
        if direction == 0:
            channels.append(jnp.cos(link_phase[direction]) * frozen)
            channels.append(jnp.sin(link_phase[direction]) * frozen)
        else:
            channels.append(jnp.cos(link_phase[direction]))
            channels.append(jnp.sin(link_phase[direction]))
    return jnp.stack(channels, axis=0)


GROUP = ("ta", "gz", "gy")
MESH = pl.DeviceIdType.MESH
F32 = jnp.float32

SPIN_K = {
    1: [[(-1, 0, 1), (1, 0, 0)], [(1, 1, 1), (-1, 1, 0)]],
    2: [[(1, 1, 0), (1, 1, 1)], [(-1, 0, 0), (-1, 0, 1)]],
    3: [[(-1, 1, 1), (1, 1, 0)], [(-1, 0, 1), (1, 0, 0)]],
}
TURN = {0: [[(-1, 0, 0), (-1, 0, 1)], [(-1, 1, 0), (-1, 1, 1)]], **SPIN_K}
BACK = {0: [[(1, 0, 0), (1, 0, 1)], [(1, 1, 0), (1, 1, 1)]], **SPIN_K}


def group_size():
    return lax.axis_size("ta") * lax.axis_size("gz") * lax.axis_size("gy")


def each(count, step):
    if count <= 16:
        for index in range(count):
            step(index)
    else:

        def looped(index, carry):
            step(index)
            return carry

        lax.fori_loop(0, count, looped, 0)


def peer(offset):
    nz, ny = lax.axis_size("gz"), lax.axis_size("gy")
    mine = (lax.axis_index("ta") * nz + lax.axis_index("gz")) * ny + lax.axis_index("gy")
    target = lax.rem(mine + offset, group_size())
    return {
        "groups": lax.axis_index("groups"),
        "ta": target // (nz * ny),
        "gz": lax.rem(target // ny, nz),
        "gy": lax.rem(target, ny),
    }


def greet_group():
    barrier = pltpu.get_barrier_semaphore()

    def greet(index):
        pl.semaphore_signal(barrier, inc=1, device_id=peer(index + 1), device_id_type=MESH)

    each(group_size() - 1, greet)


def await_group():
    pl.semaphore_wait(pltpu.get_barrier_semaphore(), group_size() - 1)


def plane_size():
    return lax.axis_size("gz") * lax.axis_size("gy")


def plane_place():
    return lax.axis_index("gz") * lax.axis_size("gy") + lax.axis_index("gy")


def plane_peer(offset):
    ny = lax.axis_size("gy")
    target = lax.rem(plane_place() + offset, plane_size())
    return {"gz": target // ny, "gy": lax.rem(target, ny)}


def time_peer(offset):
    return {"ta": lax.rem(lax.axis_index("ta") + offset, lax.axis_size("ta"))}


def greet_lines():
    barrier = pltpu.get_barrier_semaphore()
    planes, times = plane_size() - 1, lax.axis_size("ta") - 1
    for count, partner in ((planes, plane_peer), (times, time_peer)):

        def greet(index):
            pl.semaphore_signal(barrier, inc=1, device_id=partner(index + 1), device_id_type=MESH)

        each(count, greet)
    pl.semaphore_wait(barrier, planes + times)


def step_along(axis, distance):
    count = lax.axis_size(axis)
    return {axis: lax.rem(lax.axis_index(axis) + (distance + count), count)}


def rows_of(shape):
    return lax.broadcasted_iota(jnp.int32, shape, len(shape) - 2)


def lanes_of(shape):
    return lax.broadcasted_iota(jnp.int32, shape, len(shape) - 1)


def turned(tensor, shift, axis):
    size = tensor.shape[axis]
    shift = shift % size
    return tensor if shift == 0 else pltpu.roll(tensor, shift, axis)


def colour_forward(quad, half):
    a_re, a_im, b_re, b_im = quad
    result = []
    for spin in range(2):
        (u_re, u_im), (l_re, l_im) = half[spin]
        result.append(
            [
                [
                    a_re * u_re - a_im * u_im + b_re * l_re - b_im * l_im,
                    a_re * u_im + a_im * u_re + b_re * l_im + b_im * l_re,
                ],
                [
                    a_re * l_re + a_im * l_im - b_re * u_re - b_im * u_im,
                    a_re * l_im - a_im * l_re - b_re * u_im + b_im * u_re,
                ],
            ]
        )
    return result


def colour_adjoint(quad, half):
    a_re, a_im, b_re, b_im = quad
    result = []
    for spin in range(2):
        (u_re, u_im), (l_re, l_im) = half[spin]
        result.append(
            [
                [
                    a_re * u_re + a_im * u_im - b_re * l_re + b_im * l_im,
                    a_re * u_im - a_im * u_re - b_re * l_im - b_im * l_re,
                ],
                [
                    b_re * u_re + b_im * u_im + a_re * l_re - a_im * l_im,
                    b_re * u_im - b_im * u_re + a_re * l_im + a_im * l_re,
                ],
            ]
        )
    return result


def project(field, mu, sign):
    half = []
    for spin in range(2):
        colours = []
        for colour in range(2):
            parts = []
            for part in range(2):
                flip, s, r = TURN[mu][spin][part]
                upper, lower = field[spin, colour, part], field[2 + s, colour, r]
                parts.append(upper + lower if flip * sign > 0 else upper - lower)
            colours.append(parts)
        half.append(colours)
    return half


def along_x(tensor, stride):
    axis = tensor.ndim - 1
    place = lax.rem(lanes_of(tensor.shape), X_LEN)
    wrap = X_LEN - 1
    if stride > 0:
        return jnp.where(place == wrap, turned(tensor, wrap, axis), turned(tensor, -1, axis))
    return jnp.where(place == 0, turned(tensor, -wrap, axis), turned(tensor, 1, axis))


def each_part():
    return [(s, c, r) for s in range(2) for c in range(2) for r in range(2)]


def cg_kernel(
    pseudo_ref,
    gauge_ref,
    sol_ref,
    force_ref,
    links,
    bank,
    dvec,
    xs,
    es,
    out,
    hop,
    t_send,
    t_recv,
    z_send,
    z_recv,
    y_send,
    y_recv,
    f_send,
    f_recv,
    ratio,
    red_send,
    red_recv,
    halo_ssem,
    halo_rsem,
    f_ssem,
    f_rsem,
    red_ssem,
    red_rsem,
):
    greet_group()
    nt, nz, width = pseudo_ref.shape[-3:]
    shape = (2, nt * nz, width)
    others = group_size() - 1
    row, lane = rows_of(shape), lanes_of(shape)
    z_place = lax.rem(row, nz)
    t_low = row < (nt - 1) * nz
    y_count = width // X_LEN
    kappa = jnp.where(lax.broadcasted_iota(jnp.int32, shape, 0) == 0, KAPPAS[0], KAPPAS[1]).astype(F32)
    last_sign = jnp.where(lax.axis_index("ta") == lax.axis_size("ta") - 1, -1.0, 1.0).astype(F32)
    first_sign = jnp.where(lax.axis_index("ta") == 0, -1.0, 1.0).astype(F32)

    for mu in range(4):
        for part in range(4):
            for t in range(nt):
                links[mu, part, t * nz : (t + 1) * nz] = gauge_ref[mu, part, t]
    for flavour in range(2):
        for s in range(4):
            for c in range(2):
                for r in range(2):
                    for t in range(nt):
                        rows = slice(t * nz, (t + 1) * nz)
                        bank[0, s, c, r, flavour, rows] = pseudo_ref[flavour, s, c, r, t]
    for s in range(4):
        zero = jnp.zeros((2, 2) + shape, F32)
        bank[1, s] = zero
        dvec[s] = zero
        xs[s] = zero
        es[s] = zero
        out[s] = zero
    ratio[...] = jnp.ones(ratio.shape, F32)

    await_group()

    def reduce_copy(parity, index):
        return pltpu.make_async_remote_copy(
            src_ref=red_send.at[parity],
            dst_ref=red_recv.at[parity, index],
            send_sem=red_ssem.at[parity, index],
            recv_sem=red_rsem.at[parity, index],
            device_id=peer(index + 1),
            device_id_type=MESH,
        )

    def start_sum(parity, total):
        folded = total[:, :, 0:128]
        for start in range(128, width, 128):
            folded = folded + total[:, :, start : start + 128]
        sums = jnp.sum(folded, axis=1, keepdims=True)
        tile_row = rows_of((8, 128))
        red_send[parity] = jnp.where(tile_row == 0, sums[0], jnp.where(tile_row == 1, sums[1], 0.0))
        each(others, lambda index: reduce_copy(parity, index).start())

    def finish_sum(parity):
        each(others, lambda index: reduce_copy(parity, index).wait())
        total = red_send[parity] + jnp.sum(red_recv[parity], axis=0)
        total = jnp.broadcast_to(jnp.sum(total, axis=1, keepdims=True), (8, 128))
        return jnp.where(rows_of((8, 128)) < 2, total, 1.0)

    def spread(pair):
        return jnp.stack([jnp.broadcast_to(pair[f : f + 1, 0:1], shape[1:]) for f in range(2)])

    def halo_copy(side, parity):
        send, recv, axis = ((t_send, t_recv, "ta"), (z_send, z_recv, "gz"), (y_send, y_recv, "gy"))[side // 2]
        return pltpu.make_async_remote_copy(
            src_ref=send.at[side % 2],
            dst_ref=recv.at[parity, side % 2],
            send_sem=halo_ssem.at[side],
            recv_sem=halo_rsem.at[parity, side],
            device_id=step_along(axis, -1 if side % 2 == 0 else 1),
            device_id_type=MESH,
        )

    def pack_t(half, ahead, send):
        for s, c in ((0, 0), (0, 1), (1, 0), (1, 1)):
            first, second = half[s][c]
            moved = [turned(v, -nz if ahead else nz, 1) for v in (first, second)]
            if ahead:
                send[2 * s + c] = jnp.where(row < nz, second, moved[0]) if nt == 2 else None
            else:
                send[2 * s + c] = jnp.where(row < nz, moved[0], second)
            yield s, c, moved

    def place_t(halo, moved, ahead, part):
        if ahead:
            edge = halo if part == 0 else turned(halo, nz, 1)
            return jnp.where(t_low, moved, edge)
        edge = halo if part == 0 else turned(halo, nz, 1)
        return jnp.where(row < nz, edge, moved)

    def send_halos(field, parity):
        for mu in range(3):
            for back in range(2):
                half = project(field, mu, -1 if back else 1)
                if back:
                    half = colour_adjoint([links[mu, p] for p in range(4)], half)
                side = 2 * mu + back
                if mu == 0:
                    for s, c, moved in pack_t(half, not back, t_send.at[back]):
                        for r in range(2):
                            hop[side, s, c, r] = moved[r]
                elif mu == 1:
                    packed = [None, None]
                    for s, c, r in each_part():
                        value = half[s][c][r]
                        hop[side, s, c, r] = turned(value, 1 if back else -1, 1)
                        slot = 2 * s + c
                        put = turned(value, slot - (nz - 1) if back else slot, 1)
                        packed[r] = put if packed[r] is None else jnp.where(z_place == slot, put, packed[r])
                    for r in range(2):
                        z_send[back, r] = packed[r]
                else:
                    packed = None
                    for s, c, r in each_part():
                        value = half[s][c][r]
                        hop[side, s, c, r] = turned(value, X_LEN if back else -X_LEN, 2)
                        slot = 4 * s + 2 * c + r
                        put = turned(value, (slot - (y_count - 1) if back else slot) * X_LEN, 2)
                        packed = put if packed is None else jnp.where(lane // X_LEN == slot, put, packed)
                    y_send[back] = packed
                halo_copy(side, parity).start()

    def add_hop(total, half, mu, back):
        sign = 1 if back else -1
        for s, c, r in each_part():
            flip, source, part = BACK[mu][s][r]
            top, low = half[s][c][r], half[source][c][part]
            if total[s][c][r] is None:
                total[s][c][r] = top
                total[2 + s][c][r] = low if flip * sign > 0 else -low
            else:
                total[s][c][r] = total[s][c][r] + top
                lower = total[2 + s][c][r]
                total[2 + s][c][r] = lower + low if flip * sign > 0 else lower - low

    def turned_wilson(source, parity):
        field = {
            (s, c, r): bank[source, s, c, r] for s in range(4) for c in range(2) for r in range(2)
        }
        send_halos(field, parity)
        total = [[[None, None], [None, None]] for _ in range(4)]
        quad = [links[3, p] for p in range(4)]
        half = project(field, 3, 1)
        ahead = [[[along_x(half[s][c][r], 1) for r in range(2)] for c in range(2)] for s in range(2)]
        add_hop(total, colour_forward(quad, ahead), 3, False)
        half = colour_adjoint(quad, project(field, 3, -1))
        behind = [[[along_x(half[s][c][r], -1) for r in range(2)] for c in range(2)] for s in range(2)]
        add_hop(total, behind, 3, True)
        for s in range(4):
            for c in range(2):
                for r in range(2):
                    out[s, c, r] = total[s][c][r]
        for mu in (2, 1, 0):
            total = [[[out[s, c, r] for r in range(2)] for c in range(2)] for s in range(4)]
            for back in range(2):
                side = 2 * mu + back
                halo_copy(side, parity).wait()
                half = [[[None, None], [None, None]] for _ in range(2)]
                for s, c, r in each_part():
                    moved = hop[side, s, c, r]
                    if mu == 0:
                        halo = t_recv[parity, back, 2 * s + c] * (first_sign if back else last_sign)
                        merged = place_t(halo, moved, not back, r)
                    elif mu == 1:
                        slot = 2 * s + c
                        halo = z_recv[parity, back, r]
                        if back:
                            merged = jnp.where(z_place == 0, turned(halo, -slot, 1), moved)
                        else:
                            merged = jnp.where(z_place == nz - 1, turned(halo, nz - 1 - slot, 1), moved)
                    else:
                        slot = 4 * s + 2 * c + r
                        halo = y_recv[parity, back]
                        if back:
                            merged = jnp.where(lane < X_LEN, turned(halo, -slot * X_LEN, 2), moved)
                        else:
                            placed = turned(halo, (y_count - 1 - slot) * X_LEN, 2)
                            merged = jnp.where(lane >= width - X_LEN, placed, moved)
                    half[s][c][r] = merged
                if not back:
                    half = colour_forward([links[mu, p] for p in range(4)], half)
                add_hop(total, half, mu, back)
            for s in range(4):
                for c in range(2):
                    for r in range(2):
                        value = total[s][c][r]
                        if mu == 0:
                            value = bank[source, s, c, r] - kappa * value
                            value = value if s < 2 else -value
                        out[s, c, r] = value

    def iteration(k, carry):
        start_sum(0, sum(jnp.sum(bank[0, s] * bank[0, s], axis=(0, 1)) for s in range(4)))
        turned_wilson(0, 0)
        norm = finish_sum(0)
        growth = spread(jnp.where(k > 0, norm / ratio[...], 0.0))
        ratio[...] = norm
        square = jnp.zeros(shape, F32)
        for s in range(4):
            image = out[s] + growth * bank[1, s]
            bank[1, s] = image
            dvec[s] = bank[0, s] + growth * dvec[s]
            square = square + jnp.sum(image * image, axis=(0, 1))
        start_sum(1, square)

        @pl.when(k < ITERS - 1)
        def _():
            turned_wilson(1, 1)

        length = spread(ratio[...] / finish_sum(1))
        for s in range(4):
            xs[s] = xs[s] + length * dvec[s]
            es[s] = es[s] + length * bank[1, s]
            bank[0, s] = bank[0, s] - length * out[s]
        return carry

    lax.fori_loop(0, ITERS, iteration, 0)

    def front_copy(which):
        return pltpu.make_async_remote_copy(
            src_ref=f_send.at[which],
            dst_ref=f_recv.at[which],
            send_sem=f_ssem.at[which],
            recv_sem=f_rsem.at[which],
            device_id=step_along("ta", -1),
            device_id_type=MESH,
        )

    for which, held in enumerate((xs, es)):
        half = project({(s, c, r): held[s, c, r] for s in range(4) for c in range(2) for r in range(2)}, 0, 1)
        for s, c, moved in pack_t(half, True, f_send.at[which]):
            for r in range(2):
                hop[which, s, c, r] = moved[r]
        front_copy(which).start()
    for flavour in range(2):
        for s in range(4):
            for c in range(2):
                for r in range(2):
                    for t in range(nt):
                        sol_ref[flavour, s, c, r, t] = xs[s, c, r, flavour, t * nz : (t + 1) * nz]
    force = jnp.zeros(shape, F32)
    for which, held in enumerate((es, xs)):
        front_copy(which).wait()
        half = [[[None, None], [None, None]] for _ in range(2)]
        for s, c, r in each_part():
            half[s][c][r] = place_t(f_recv[which, 2 * s + c] * last_sign, hop[which, s, c, r], True, r)
        image = colour_forward([links[0, p] for p in range(4)], half)
        for s in range(2):
            for c in range(2):
                left = [held[s, c, r] + held[2 + s, c, r] for r in range(2)]
                term = left[1] * image[s][c][0] - left[0] * image[s][c][1]
                force = force + term if c == 0 else force - term
    force = force * (2.0 * kappa)
    force = force[0] + force[1]
    for t in range(nt):
        force_ref[t] = force[t * nz : (t + 1) * nz]


def conjugate_gradient(pseudo, gauge):
    nt, nz, width = pseudo.shape[1:]
    rows = nt * nz
    others = group_size() - 1
    field = (4, 2, 2, 2, rows, width)
    vmem = lambda *dims: pltpu.VMEM(dims, F32)
    dma = lambda *dims: pltpu.SemaphoreType.DMA(dims)
    sol, force = pl.pallas_call(
        cg_kernel,
        out_shape=(
            jax.ShapeDtypeStruct((2, 4, 2, 2, nt, nz, width), F32),
            jax.ShapeDtypeStruct((nt, nz, width), F32),
        ),
        in_specs=[pl.BlockSpec(memory_space=pltpu.VMEM)] * 2,
        out_specs=[pl.BlockSpec(memory_space=pltpu.VMEM)] * 2,
        scratch_shapes=[
            vmem(4, 4, rows, width),
            vmem(2, *field),
            vmem(*field),
            vmem(*field),
            vmem(*field),
            vmem(*field),
            vmem(6, 2, 2, 2, 2, rows, width),
            vmem(2, 4, 2, rows, width),
            vmem(2, 2, 4, 2, rows, width),
            vmem(2, 2, 2, rows, width),
            vmem(2, 2, 2, 2, rows, width),
            vmem(2, 2, rows, width),
            vmem(2, 2, 2, rows, width),
            vmem(2, 4, 2, rows, width),
            vmem(2, 4, 2, rows, width),
            vmem(8, 128),
            vmem(2, 8, 128),
            vmem(2, others, 8, 128),
            dma(6),
            dma(2, 6),
            dma(2),
            dma(2),
            dma(2, others),
            dma(2, others),
        ],
        compiler_params=pltpu.CompilerParams(
            collective_id=0, has_side_effects=True, vmem_limit_bytes=32 * 1024 * 1024
        ),
    )(pseudo.reshape((2, 4, 2, 2, nt, nz, width)), gauge.reshape((4, 4, nt, nz, width)))
    return sol.reshape(pseudo.shape), force


def sum_kernel(data_ref, out_ref, landed, lined, reduced, *sems):
    planes, times = plane_size(), lax.axis_size("ta")
    chunk = data_ref.shape[0] // planes
    place, now = plane_place(), lax.axis_index("ta")
    greet_lines()

    def part_of(device):
        return pl.ds(pl.multiple_of(device * chunk, 8), chunk)

    def copy(stage, index, src, dst, target):
        return pltpu.make_async_remote_copy(
            src_ref=src,
            dst_ref=dst,
            send_sem=sems[2 * stage].at[index],
            recv_sem=sems[2 * stage + 1].at[index],
            device_id=target,
            device_id_type=MESH,
        )

    def scatter(index):
        src = data_ref.at[part_of(lax.rem(place + index + 1, planes))]
        return copy(0, index, src, landed.at[index], plane_peer(index + 1))

    def across(index, owner):
        return copy(1, index, reduced.at[0], lined.at[owner], time_peer(index + 1))

    def gather(index, owner):
        return copy(2, index, reduced.at[1], out_ref.at[part_of(owner)], plane_peer(index + 1))

    each(planes - 1, lambda index: scatter(index).start())
    each(planes - 1, lambda index: scatter(index).wait())
    partial = data_ref[part_of(place)] + jnp.sum(landed[...], axis=0)
    reduced[0] = partial
    each(times - 1, lambda index: across(index, now).start())
    lined[now] = partial
    each(times - 1, lambda index: across(index, lax.rem(now + times - index - 1, times)).wait())
    total = jnp.sum(lined[...], axis=0)
    reduced[1] = total
    each(planes - 1, lambda index: gather(index, place).start())
    out_ref[part_of(place)] = total
    each(planes - 1, lambda index: gather(index, lax.rem(place + planes - index - 1, planes)).wait())


def group_sum(table):
    planes, times = plane_size(), lax.axis_size("ta")
    tiles = table.reshape((2, 8, 8, 128)).transpose((0, 2, 1, 3)).reshape((128, 128))
    chunk = -(-16 // planes) * 8
    data = jnp.pad(tiles, ((0, planes * chunk - 128), (0, 0)))
    counts = (planes - 1, planes - 1, times - 1, times - 1, planes - 1, planes - 1)
    summed = pl.pallas_call(
        sum_kernel,
        out_shape=jax.ShapeDtypeStruct(data.shape, F32),
        in_specs=[pl.BlockSpec(memory_space=pltpu.VMEM)],
        out_specs=pl.BlockSpec(memory_space=pltpu.VMEM),
        scratch_shapes=[
            pltpu.VMEM((planes - 1, chunk, 128), F32),
            pltpu.VMEM((times, chunk, 128), F32),
            pltpu.VMEM((2, chunk, 128), F32),
            *[pltpu.SemaphoreType.DMA((count,)) for count in counts],
        ],
        compiler_params=pltpu.CompilerParams(
            collective_id=1, has_side_effects=True, vmem_limit_bytes=32 * 1024 * 1024
        ),
    )(data)
    return summed[:128].reshape((2, 8, 8, 128)).transpose((0, 2, 1, 3)).reshape((16, 1024))


def tap_kernel(feature_ref, taps_ref, ext, ssem, rsem):
    nt, nz, channels, width = feature_ref.shape
    edge = 128
    for t in range(nt):
        for z in range(nz):
            ext[1 + t, 1 + z, :, edge : edge + width] = feature_ref[t, z]
    greet_lines()

    def swap(index, axis, low, low_halo, high, high_halo):
        copies = []
        for side, (src, dst) in enumerate(((low, high_halo), (high, low_halo))):
            copies.append(
                pltpu.make_async_remote_copy(
                    src_ref=src,
                    dst_ref=dst,
                    send_sem=ssem.at[2 * index + side],
                    recv_sem=rsem.at[2 * index + side],
                    device_id=step_along(axis, 1 if side else -1),
                    device_id_type=MESH,
                )
            )
        for copy in copies:
            copy.start()
        for copy in copies:
            copy.wait()

    body = pl.ds(edge, width)
    mid = pl.ds(1, nz)
    swap(
        0,
        "ta",
        ext.at[1, mid, :, body],
        ext.at[0, mid, :, body],
        ext.at[nt, mid, :, body],
        ext.at[nt + 1, mid, :, body],
    )
    swap(
        1,
        "gz",
        ext.at[:, 1, :, body],
        ext.at[:, 0, :, body],
        ext.at[:, nz, :, body],
        ext.at[:, nz + 1, :, body],
    )
    swap(
        2,
        "gy",
        ext.at[:, :, :, pl.ds(edge, edge)],
        ext.at[:, :, :, pl.ds(0, edge)],
        ext.at[:, :, :, pl.ds(width, edge)],
        ext.at[:, :, :, pl.ds(edge + width, edge)],
    )
    for tt in range(nt + 2):
        for zz in range(nz + 2):
            cells = ext[tt, zz]
            for oy in (-1, 0, 1):
                base = turned(cells, -(edge + X_LEN * oy), 1)[:, 0:width]
                for ox in (-1, 0, 1):
                    tile = base if ox == 0 else along_x(base, ox)
                    for ot in (-1, 0, 1):
                        for oz in (-1, 0, 1):
                            t, z = tt - 1 - ot, zz - 1 - oz
                            if 0 <= t < nt and 0 <= z < nz:
                                tap = 27 * (ot + 1) + 9 * (oz + 1) + 3 * (oy + 1) + ox + 1
                                start = (t * nz + z) * width
                                taps_ref[tap * channels : (tap + 1) * channels, start : start + width] = tile


def conditioner_taps(features):
    nt, nz, channels, width = features.shape
    return pl.pallas_call(
        tap_kernel,
        out_shape=jax.ShapeDtypeStruct((81 * channels, nt * nz * width), F32),
        in_specs=[pl.BlockSpec(memory_space=pltpu.VMEM)],
        out_specs=pl.BlockSpec(memory_space=pltpu.VMEM),
        scratch_shapes=[
            pltpu.VMEM((nt + 2, nz + 2, channels, width + 256), F32),
            pltpu.SemaphoreType.DMA((6,)),
            pltpu.SemaphoreType.DMA((6,)),
        ],
        compiler_params=pltpu.CompilerParams(
            collective_id=2, has_side_effects=True, vmem_limit_bytes=32 * 1024 * 1024
        ),
    )(features)


def on_device(pseudo, frame_quat, link_phase, active, kernel, bias_hidden, readout, bias_out):
    scale = SLOPE_SHARE * 2.0 * math.pi / KNOTS
    ratio = KNOTS / (2.0 * math.pi)
    mask = active.astype(F32).reshape((-1,))
    taps = conditioner_taps(conditioner_inputs(link_phase, active).transpose((1, 2, 0, 3)))
    summed = jnp.einsum("ti,ts->is", kernel, taps, precision=lax.Precision.HIGH)
    hidden = jnp.tanh(summed + bias_hidden[:, None])
    logits = jnp.einsum("ik,is->ks", readout, hidden, precision=PRECISE)
    squashed = jnp.tanh(logits + bias_out[:, None])
    coeffs = scale * squashed
    angle = link_phase[0].reshape((-1,))
    values, slopes = spline_basis(angle)
    moved = angle + mask * jnp.sum(coeffs * values, axis=0)
    jacobian = 1.0 + mask * ratio * jnp.sum(coeffs * slopes, axis=0)
    angles = jnp.concatenate([moved.reshape((1,) + active.shape), link_phase[1:]], axis=0)
    solution, force_field = conjugate_gradient(pseudo, rotate_links(frame_quat, angles))
    root_volume = math.sqrt(active.size * group_size())
    force = force_field.reshape((-1,))
    coeff_grad = mask * (force * values - ratio * slopes / jacobian) / root_volume
    logit_grad = coeff_grad * scale * (1.0 - squashed * squashed)
    pre_grad = jnp.einsum("ik,ks->is", readout, logit_grad, precision=PRECISE) * (1.0 - hidden * hidden)
    kernel_part = jnp.einsum("is,ts->it", pre_grad, taps, precision=lax.Precision.HIGH)
    readout_part = jnp.einsum("is,ks->ik", hidden, logit_grad, precision=PRECISE)
    hidden_part = jnp.sum(pre_grad, axis=1, keepdims=True)
    out_part = jnp.pad(jnp.sum(logit_grad, axis=1, keepdims=True), ((0, 16 - KNOTS), (0, 0)))
    n = kernel.shape[0]
    table = jnp.concatenate([kernel_part, readout_part, hidden_part, out_part], axis=1)
    table = group_sum(jnp.pad(table, ((0, 0), (0, 1024 - table.shape[1]))))
    return (
        solution,
        force_field,
        table[:, :n].T,
        table[:, n + KNOTS],
        table[:, n : n + KNOTS],
        table[:KNOTS, n + KNOTS + 1],
    )


def solution(mesh):
    return jax.shard_map(
        on_device,
        mesh=mesh,
        in_specs=(
            P("groups", "ta", "gz", "gy"),
            P("groups", "ta", "gz", "gy"),
            P("groups", "ta", "gz", "gy"),
            P(("groups", "ta"), "gz", "gy"),
            P(),
            P(),
            P(),
            P(),
        ),
        out_specs=(
            P("groups", "ta", "gz", "gy"),
            P(("groups", "ta"), "gz", "gy"),
            P("groups", None),
            P("groups"),
            P("groups", None),
            P("groups"),
        ),
        check_vma=False,
    )
```
